32 devices in a mesh: groups: 2 (over x), ctx: 16 (over z, y, core).
Axes of the slice: x: 2, y: 2, z: 4, core: 2. Of those that a mesh axis runs over, the one named last changes fastest.
Arguments:
- residual: bfloat16 [4096, 2048], P(('groups', 'ctx')), parts along dimension 0, may hold values from -200 to 200
- queries: bfloat16 [4096, 2048], P(('groups', 'ctx')), parts along dimension 0, may hold values from -64 to 64
- keys: bfloat16 [4096, 256], P(('groups', 'ctx')), parts along dimension 0, may hold values from -64 to 64
- values: bfloat16 [4096, 256], P(('groups', 'ctx')), parts along dimension 0, may hold values from -6 to 6
- block_order: int32 [32], P('groups'), parts along dimension 0, may hold values from 0 to 3, as said below
- routes: int32 [4096, 8], P(('groups', 'ctx')), parts along dimension 0, may hold values from 0 to 15, as said below
- route_weights: float32 [4096, 8], P(('groups', 'ctx')), parts along dimension 0, may hold values from 0.1 to 1
- out_weight: bfloat16 [2048, 2048], P(None, 'ctx'), may hold values from -0.125 to 0.125
- norm_gain: float32 [2048], replicated, may hold values from 0.5 to 1.5
- w_gate_up: bfloat16 [16, 2048, 1536], P('ctx'), may hold values from -0.125 to 0.125
- w_down: bfloat16 [16, 768, 2048], P('ctx'), may hold values from -0.21875 to 0.21875
Outputs:
- context: bfloat16 [4096, 2048], P(('groups', 'ctx')), parts along dimension 0
- mixed: bfloat16 [4096, 2048], P(('groups', 'ctx')), parts along dimension 0
The draws below stay inside these ranges and needn't reach their ends.
There are 2 independent parts, one for each index of `groups`. The reference program is written for one: setup_inputs(seed, part) draws one part's arguments, and reference() takes and returns one part's arrays. A program takes and returns all parts, laid end to end along the dimension named above; an argument that names none is the same for every part. Nothing has to cross between parts.
Inputs may be any that keep to these rules, and one draw needn't show every extreme that they name: `block_order`: for each i below 4, the entries at the indices congruent to i modulo 4 hold every number from 0 to 3 once. `routes`: each token names 8 different experts. Among the tokens of one device no expert is named more than 72 times, and some expert is named exactly 72 times by the tokens of every device.
All inputs are finite; a program needn't handle non-finite values.
Results may differ from the reference program's by a relative error of at most 0.005.
Values may be sent and summed in bfloat16 or wider, within the bound.
A program may use at most 128 MiB of HBM per device.

```python
import jax
import jax.numpy as jnp
from jax import lax

D = 2048
HEAD_SIZE = 128
FF = 768
QUERY_HEADS = 16
KEY_VALUE_HEADS = 2
TOPK = 8
SEQS = 4
DEVICE_TOKENS = 128
EXPERTS = 16
SPAN = 4
PROMPT_LENGTH = 512
TOKEN_COUNT = 2048
MOST = 72
N_CTX = 16


def query_key_pair(key):
    query_key = jax.random.fold_in(key, 11)
    random_key_draw = jax.random.fold_in(key, 12)
    query_rows = jnp.clip(jax.random.normal(query_key, (TOKEN_COUNT, QUERY_HEADS * HEAD_SIZE), jnp.float32), -6.0, 6.0)
    key_row_matrix = jnp.clip(jax.random.normal(random_key_draw, (TOKEN_COUNT, KEY_VALUE_HEADS * HEAD_SIZE), jnp.float32), -6.0, 6.0)
    return (query_rows, key_row_matrix)


def draw_queries(key, part):
    return query_key_pair(key)[0].astype(jnp.bfloat16)


def draw_keys(key, part):
    return query_key_pair(key)[1].astype(jnp.bfloat16)


def draw_residual(key, part):
    values_out = jnp.clip(jax.random.normal(jax.random.fold_in(key, 41), (TOKEN_COUNT, D), jnp.float32), -6.0, 6.0)
    return values_out.astype(jnp.bfloat16)


def draw_block_order(key, part):
    span = TOKEN_COUNT // DEVICE_TOKENS // SEQS
    prompt_key_rows = jax.random.split(jax.random.fold_in(key, 31), SEQS)
    orders = jax.vmap(lambda single: jax.random.permutation(single, span))(prompt_key_rows)
    return orders.T.reshape(-1).astype(jnp.int32)


def draw_routes(key, part):
    blocks = TOKEN_COUNT // DEVICE_TOKENS
    slots = EXPERTS * MOST
    total = DEVICE_TOKENS * TOPK
    favour = jax.random.randint(jax.random.fold_in(key, 21), (EXPERTS,), 0, 4)
    busiest = jax.random.randint(jax.random.fold_in(key, 22), (), 0, EXPERTS)
    favour = jnp.where(jnp.arange(EXPERTS) == busiest, 8, favour)
    slot_ids = jnp.arange(slots)

    def one_block(index):
        block_key = jax.random.fold_in(jax.random.fold_in(key, 23), index)
        noise = jax.random.randint(block_key, (slots,), 0, 65536)
        priority = (favour[slot_ids // MOST] * 65536 + noise) * slots + slot_ids
        unused, picked = lax.top_k(priority, total)
        chosen = jnp.sort(picked) // MOST
        table = chosen.reshape(TOPK, DEVICE_TOKENS).T
        shuffle = jax.random.permutation(jax.random.fold_in(block_key, 1), DEVICE_TOKENS)
        return table[shuffle]
    return jax.vmap(one_block)(jnp.arange(blocks)).reshape(TOKEN_COUNT, TOPK).astype(jnp.int32)


def steps_of(own_key, extent, cuts, smallest, high):
    def one(dim, parts):
        steps = jax.random.uniform(jax.random.fold_in(jax.random.fold_in(own_key, 6), dim), (parts,), jnp.float32, smallest / len(cuts), high / len(cuts))
        return jnp.repeat(jnp.exp(steps), extent[dim] // parts).reshape((-1,) + (1,) * (len(extent) - dim - 1))

    level = one(*cuts[0])
    for cut in cuts[1:]:
        level = level * one(*cut)
    return level


def gaussian(own_key, shape, scale, reach, cuts=(), kind=jnp.bfloat16):
    factor_of = steps_of(own_key, shape, cuts, -0.22, 0.18) if cuts else 1.0
    drawn = jax.random.normal(own_key, shape, jnp.float32) * scale * factor_of
    return jnp.minimum(jnp.maximum(drawn, -reach), reach).astype(kind)


def setup_inputs(seed: int = 0, part: int = 0) -> dict:
    key_list = jax.random.split(jax.random.key(seed), 12)
    own_keys = jax.random.split(jax.random.fold_in(key_list[11], part), 12)
    residual = draw_residual(jax.random.fold_in(jax.random.fold_in(key_list[11], part), 71), part)
    queries = draw_queries(jax.random.fold_in(jax.random.fold_in(key_list[11], part), 71), part)
    keys = draw_keys(jax.random.fold_in(jax.random.fold_in(key_list[11], part), 71), part)
    values = gaussian(own_keys[3], (TOKEN_COUNT, KEY_VALUE_HEADS * HEAD_SIZE), 1.0, 6.0, ((0, 16),))
    block_order = draw_block_order(jax.random.fold_in(jax.random.fold_in(key_list[11], part), 71), part)
    routes = draw_routes(jax.random.fold_in(jax.random.fold_in(key_list[11], part), 71), part)
    route_weights = jnp.clip(0.1 + 0.9 * jax.random.uniform(own_keys[6], (TOKEN_COUNT, TOPK), jnp.float32) ** steps_of(own_keys[6], (TOKEN_COUNT, TOPK), ((0, 16),), -0.2, 0.2), 0.1, 1.0)
    out_weight = gaussian(key_list[7], (QUERY_HEADS * HEAD_SIZE, D), (QUERY_HEADS * HEAD_SIZE) ** -0.5, 0.125, ((1, 16),))
    norm_gain = jnp.clip(1.0 + 0.1 * jax.random.normal(key_list[8], (D,), jnp.float32), 0.5, 1.5)
    w_gate_up = gaussian(key_list[9], (EXPERTS, D, 2 * FF), D ** -0.5, 0.125, ((0, 16),))
    w_down = gaussian(key_list[10], (EXPERTS, FF, D), FF ** -0.5, 0.21875, ((0, 16),))
    return dict(residual=residual, queries=queries, keys=keys, values=values, block_order=block_order, routes=routes, route_weights=route_weights, out_weight=out_weight, norm_gain=norm_gain, w_gate_up=w_gate_up, w_down=w_down)


def attend_prompt(prompt_queries, prompt_key_rows, prompt_value_rows, prompt_positions):
    query_group_width = QUERY_HEADS // KEY_VALUE_HEADS
    gathered_keys = prompt_key_rows.reshape(PROMPT_LENGTH, KEY_VALUE_HEADS, HEAD_SIZE).astype(jnp.float32)
    gathered_values = prompt_value_rows.reshape(PROMPT_LENGTH, KEY_VALUE_HEADS, HEAD_SIZE).astype(jnp.float32)

    def one_block(inputs):
        local_query_block, query_positions = inputs
        query_head_rows = local_query_block.reshape(DEVICE_TOKENS, KEY_VALUE_HEADS, query_group_width, HEAD_SIZE).astype(jnp.float32)
        scores = jnp.einsum('qhgd,khd->hgqk', query_head_rows, gathered_keys) * HEAD_SIZE ** (-0.5)
        visible = prompt_positions[None, :] <= query_positions[:, None]
        scores = jnp.where(visible[None, None], scores, -jnp.inf)
        highest = lax.optimization_barrier(jnp.max(scores, axis=-1, keepdims=True))
        weights = jnp.exp(scores - highest)
        totals = lax.optimization_barrier(jnp.sum(weights, axis=-1, keepdims=True))
        rounded = lax.optimization_barrier(weights.astype(jnp.bfloat16)).astype(jnp.float32)
        summed = jnp.einsum('hgqk,khd->hgqd', rounded, gathered_values) / totals
        return summed.transpose(2, 0, 1, 3).reshape(DEVICE_TOKENS, QUERY_HEADS * HEAD_SIZE).astype(jnp.bfloat16)
    return lax.map(one_block, (prompt_queries.reshape(SPAN, DEVICE_TOKENS, QUERY_HEADS * HEAD_SIZE), prompt_positions.reshape(SPAN, DEVICE_TOKENS)))

def select_rows(array, prompt):
    width = array.shape[-1]
    return array.reshape(SPAN, SEQS, DEVICE_TOKENS, width)[:, prompt].reshape(PROMPT_LENGTH, width)

def reference(residual, queries, keys, values, block_order, routes, route_weights, out_weight, norm_gain, w_gate_up, w_down):
    positions = block_order.astype(jnp.int32)[:, None] * DEVICE_TOKENS + jnp.arange(DEVICE_TOKENS, dtype=jnp.int32)[None, :]
    results = []
    for prompt in range(SEQS):
        prompt_positions = positions.reshape(SPAN, SEQS, DEVICE_TOKENS)[:, prompt].reshape(PROMPT_LENGTH)
        results.append(attend_prompt(select_rows(queries, prompt), select_rows(keys, prompt), select_rows(values, prompt), prompt_positions))
    context = jnp.stack(results, axis=1).reshape(TOKEN_COUNT, QUERY_HEADS * HEAD_SIZE)
    projected = jnp.dot(context, out_weight, preferred_element_type=jnp.float32)
    updated = residual.astype(jnp.float32) + projected
    normed = (updated * lax.rsqrt(lax.optimization_barrier(jnp.mean(updated * updated, axis=-1, keepdims=True)) + 1e-06) * norm_gain).astype(jnp.bfloat16)
    capacity = N_CTX * MOST
    expert_ids = routes.reshape(-1).astype(jnp.int32)
    one_hot = (expert_ids[:, None] == jnp.arange(EXPERTS, dtype=jnp.int32)[None, :]).astype(jnp.int32)
    ranks = lax.optimization_barrier(jnp.sum(jnp.cumsum(one_hot, axis=0) * one_hot, axis=1)) - 1
    target = expert_ids * capacity + ranks
    source_row = jnp.arange(TOKEN_COUNT * TOPK, dtype=jnp.int32) // TOPK
    table = jnp.zeros((EXPERTS * capacity,), jnp.int32).at[target].set(source_row).reshape(EXPERTS, capacity)

    def run_expert(inputs):
        gate_up, down, index_rows = inputs
        rows_in = normed[index_rows]
        both = jnp.dot(rows_in, gate_up, preferred_element_type=jnp.float32)
        hidden = (jax.nn.silu(both[:, :FF]) * both[:, FF:]).astype(jnp.bfloat16)
        return jnp.dot(hidden, down, preferred_element_type=jnp.float32).astype(jnp.bfloat16)
    outputs = lax.map(run_expert, (w_gate_up, w_down, table))
    gathered = outputs.reshape(EXPERTS * capacity, D)[target].reshape(TOKEN_COUNT, TOPK, D)
    gates = route_weights / lax.optimization_barrier(jnp.sum(route_weights, axis=-1, keepdims=True))
    mixed = updated
    for slot in range(TOPK):
        mixed = mixed + gates[:, slot:slot + 1] * gathered[:, slot].astype(jnp.float32)
    return (context, mixed.astype(jnp.bfloat16))
```

```python
import functools

import jax
import jax.numpy as jnp
from jax import lax
from jax.experimental import pallas as pl
from jax.experimental.pallas import tpu as pltpu
from jax.sharding import PartitionSpec as P

D = 2048
HEAD_SIZE = 128
FF = 768
QUERY_HEADS = 16
KEY_VALUE_HEADS = 2
TOPK = 8
SEQS = 4


def shifted(array, axis, by):
    devices = lax.axis_size(axis)
    return lax.ppermute(array, axis, [(i, (i + by) % devices) for i in range(devices)])


VMEM_BYTES = 60 * 2**20


def put(src, dst, send_sem, recv_sem, to):
    return pltpu.make_async_remote_copy(
        src_ref=src,
        dst_ref=dst,
        send_sem=send_sem,
        recv_sem=recv_sem,
        device_id={"ctx": to},
        device_id_type=pl.DeviceIdType.MESH,
    )


def plane_at(step, z, planes):
    short = jnp.minimum(z, planes - 1 - z)
    sign = jnp.where(2 * z < planes - 1, 1, -1)
    near = (step + 1) // 2 * (2 * (step % 2) - 1)
    return z + sign * jnp.where(step <= 2 * short, near, step - short)


def expert_kernel(
    planes,
    cap,
    normed_ref,
    updated_ref,
    gates_ref,
    up_hbm,
    down_hbm,
    out_ref,
    rows_all,
    contrib,
    from_core,
    from_y,
    from_z,
    w_up,
    w_down,
    ranks,
    picked,
    act,
    w_sem,
    recv,
    up_s,
    dn_s,
    y_s,
    c_s,
    rc_s,
    rc_r,
    ry_s,
    ry_r,
    rz_s,
    rz_r,
):
    n, width = normed_ref.shape
    hidden = w_down.shape[0]
    pair = 2 * n
    me = lax.axis_index("ctx")
    z, place = me // SEQS, me % SEQS
    y, c = place // 2, place % 2
    at_y = z * SEQS + (1 - y) * 2 + c
    at_core = z * SEQS + y * 2 + (1 - c)
    above, below = z < planes - 1, z > 0

    def block(ref, index):
        return ref.at[pl.ds(pl.multiple_of(index * n, n), n)]

    load_up = pltpu.make_async_copy(up_hbm.at[0], w_up, w_sem.at[0])
    load_down = pltpu.make_async_copy(down_hbm.at[0], w_down, w_sem.at[1])
    load_up.start()
    load_down.start()

    barrier = pltpu.get_barrier_semaphore()

    def greet(to):
        pl.semaphore_signal(
            barrier, inc=1, device_id={"ctx": to}, device_id_type=pl.DeviceIdType.MESH
        )

    greet(at_y)
    greet(at_core)
    pl.when(above)(lambda: greet(me + SEQS))
    pl.when(below)(lambda: greet(me - SEQS))
    block(rows_all, me)[...] = normed_ref[...]
    pl.semaphore_wait(barrier, 2 + jnp.where(above, 1, 0) + jnp.where(below, 1, 0))

    def gather_copy(index, sem, to):
        return put(block(rows_all, index), block(rows_all, index), sem, recv.at[index], to)

    def forwards(p):
        index = p * SEQS + place
        return (
            (above & (p <= z), gather_copy(index, up_s.at[p], me + SEQS)),
            (below & (p >= z), gather_copy(index, dn_s.at[p], me - SEQS)),
            (None, gather_copy(index, y_s.at[p], at_y)),
            (None, gather_copy(index, c_s.at[p * 2 + y], at_core)),
        )

    def second_forward(p):
        return gather_copy(p * SEQS + (1 - y) * 2 + c, c_s.at[p * 2 + 1 - y], at_core)

    def core_return(p, row):
        return put(
            block(contrib, p * SEQS + row * 2 + 1 - c),
            block(from_core, p * 2 + row),
            rc_s.at[p * 2 + row],
            rc_r.at[p * 2 + row],
            at_core,
        )

    def y_return(p):
        return put(
            block(contrib, p * SEQS + (1 - y) * 2 + c),
            block(from_y, p),
            ry_s.at[p],
            ry_r.at[p],
            at_y,
        )

    def z_return(p, slot, to):
        return put(
            block(contrib, p * SEQS + place), block(from_z, slot), rz_s.at[p], rz_r.at[slot], to
        )

    shape = (pair, pair)
    earlier = lax.broadcasted_iota(jnp.int32, shape, 0)
    later = lax.broadcasted_iota(jnp.int32, shape, 1)
    before = (earlier < later) & (earlier // n == later // n)
    routed = gates_ref[...] > 0
    count = jnp.dot(
        routed.astype(jnp.bfloat16), before.astype(jnp.bfloat16), preferred_element_type=jnp.float32
    ).astype(jnp.int32)
    offset = lax.broadcasted_iota(jnp.int32, count.shape, 1) // n * cap
    ranks[...] = jnp.where(routed, count + offset, -1)

    def compute(p):
        parts = []
        for half in range(2):
            row = pl.ds(p * 2 + half, 1)
            hit = lax.broadcasted_iota(jnp.int32, (2 * cap, pair), 0) == ranks[row, :]
            gate = jnp.sum(jnp.where(hit, gates_ref[row, :], 0.0), axis=1, keepdims=True)
            choose = hit.astype(jnp.float32).astype(jnp.bfloat16)
            parts.append((choose, gate))
        tile = 512

        def pick(j, carry):
            cols = pl.ds(pl.multiple_of(j * tile, tile), tile)
            for half in range(2):
                source = pl.ds(pl.multiple_of((p * 2 + half) * pair, pair), pair)
                picked[pl.ds(half * 2 * cap, 2 * cap), cols] = jnp.dot(
                    parts[half][0], rows_all[source, cols], preferred_element_type=jnp.float32
                ).astype(jnp.bfloat16)
            return carry

        lax.fori_loop(0, width // tile, pick, 0)
        narrow = 256

        def gate_up(j, carry):
            first = pl.ds(pl.multiple_of(j * narrow, narrow), narrow)
            second = pl.ds(pl.multiple_of(hidden + j * narrow, narrow), narrow)
            v = jnp.dot(picked[...], w_up[:, first], preferred_element_type=jnp.float32)
            u = jnp.dot(picked[...], w_up[:, second], preferred_element_type=jnp.float32)
            act[:, first] = (v / (1.0 + jnp.exp(-v)) * u).astype(jnp.bfloat16)
            return carry

        lax.fori_loop(0, hidden // narrow, gate_up, 0)

        def down(j, carry):
            cols = pl.ds(pl.multiple_of(j * tile, tile), tile)
            for half in range(2):
                choose, gate = parts[half]
                source = pl.ds(pl.multiple_of((p * 2 + half) * pair, pair), pair)
                result = jnp.dot(
                    act[pl.ds(half * 2 * cap, 2 * cap), :],
                    w_down[:, cols],
                    preferred_element_type=jnp.float32,
                )
                contrib[source, cols] = lax.dot_general(
                    choose,
                    (result * gate).astype(jnp.bfloat16),
                    (((0,), (0,)), ((), ())),
                    preferred_element_type=jnp.float32,
                ).astype(jnp.bfloat16)
            return carry

        lax.fori_loop(0, width // tile, down, 0)

    def advance(k, carry):
        @pl.when(k < planes)
        def _():
            p = plane_at(k, z, planes)

            @pl.when(k > 0)
            def _():
                gather_copy(p * SEQS + place, y_s.at[p], at_y).wait_recv()

            for condition, copy in forwards(p):
                if condition is None:
                    copy.start()
                else:
                    pl.when(condition)(copy.start)

        @pl.when(k > 0)
        def _():
            p = plane_at(k - 1, z, planes)
            second_forward(p).wait_recv()
            second_forward(p).start()
            for row in range(2):
                gather_copy(p * SEQS + row * 2 + 1 - c, c_s.at[0], at_core).wait_recv()

            @pl.when(k == 1)
            def _():
                load_up.wait()
                load_down.wait()

            compute(p)
            for row in range(2):
                core_return(p, row).start()

        return carry

    lax.fori_loop(0, planes + 1, advance, 0)
    chunk = 16

    def add_up(target, terms):
        def some(i, carry):
            here = pl.ds(pl.multiple_of(i * chunk, chunk), chunk)
            total = terms[0][here, :].astype(jnp.float32)
            for term in terms[1:]:
                total = total + term[here, :].astype(jnp.float32)
            target[here, :] = total.astype(target.dtype)
            return carry

        lax.fori_loop(0, n // chunk, some, 0)

    def core_sum(i, carry):
        p = plane_at(planes - 1 - i, z, planes)
        for row in range(2):
            core_return(p, row).wait_recv()
        other = block(contrib, p * SEQS + (1 - y) * 2 + c)
        add_up(other, [other, block(from_core, p * 2 + 1 - y)])
        y_return(p).start()
        return carry

    lax.fori_loop(0, planes, core_sum, 0)

    def chain(i, carry):
        p = plane_at(planes - 1 - i, z, planes)
        y_return(p).wait_recv()
        own = block(contrib, p * SEQS + place)
        add_up(own, [own, block(from_core, p * 2 + y), block(from_y, p)])

        @pl.when(((p < z) & above) | ((p > z) & below))
        def _():
            z_return(p, p, at_y).wait_recv()
            add_up(own, [own, block(from_z, p)])

        @pl.when(p < z)
        def _():
            z_return(p, jnp.where(p == z - 1, planes, p), me - SEQS).start()

        @pl.when(p > z)
        def _():
            z_return(p, p, me + SEQS).start()

        return carry

    lax.fori_loop(0, planes - 1, chain, 0)
    y_return(z).wait_recv()
    mine = block(contrib, me)
    terms = [updated_ref, mine, block(from_core, z * 2 + y), block(from_y, z)]
    low, high = block(from_z, z), block(from_z, planes)
    pl.when(below)(lambda: z_return(z, z, at_y).wait_recv())
    pl.when(above)(lambda: z_return(z, planes, at_y).wait_recv())
    pl.when(below & above)(lambda: add_up(out_ref, terms + [low, high]))
    pl.when(below & jnp.logical_not(above))(lambda: add_up(out_ref, terms + [low]))
    pl.when(jnp.logical_not(below) & above)(lambda: add_up(out_ref, terms + [high]))

    def finish(p, carry):
        for condition, copy in forwards(p):
            if condition is None:
                copy.wait_send()
            else:
                pl.when(condition)(copy.wait_send)
        second_forward(p).wait_send()
        for row in range(2):
            core_return(p, row).wait_send()
        y_return(p).wait_send()
        pl.when(p != z)(lambda: z_return(p, p, at_y).wait_send())
        return carry

    lax.fori_loop(0, planes, finish, 0)


def expert_call(normed, updated, gates_here, w_gate_up, w_down, cap):
    n, width = normed.shape
    hidden = w_down.shape[1]
    devices = lax.axis_size("ctx")
    planes = devices // SEQS
    vmem = pl.BlockSpec(memory_space=pltpu.VMEM)
    anywhere = pl.BlockSpec(memory_space=pl.ANY)
    bf16 = jnp.bfloat16
    return pl.pallas_call(
        functools.partial(expert_kernel, planes, cap),
        out_shape=jax.ShapeDtypeStruct((n, width), bf16),
        in_specs=[vmem, vmem, vmem, anywhere, anywhere],
        out_specs=vmem,
        scratch_shapes=[
            pltpu.VMEM((devices * n, width), bf16),
            pltpu.VMEM((devices * n, width), bf16),
            pltpu.VMEM((2 * planes * n, width), bf16),
            pltpu.VMEM((planes * n, width), bf16),
            pltpu.VMEM(((planes + 1) * n, width), bf16),
            pltpu.VMEM(w_gate_up.shape[1:], bf16),
            pltpu.VMEM(w_down.shape[1:], bf16),
            pltpu.VMEM((2 * planes, 2 * n), jnp.int32),
            pltpu.VMEM((SEQS * cap, width), bf16),
            pltpu.VMEM((SEQS * cap, hidden), bf16),
            pltpu.SemaphoreType.DMA((2,)),
            pltpu.SemaphoreType.DMA((devices,)),
            pltpu.SemaphoreType.DMA((planes,)),
            pltpu.SemaphoreType.DMA((planes,)),
            pltpu.SemaphoreType.DMA((planes,)),
            pltpu.SemaphoreType.DMA((2 * planes,)),
            pltpu.SemaphoreType.DMA((2 * planes,)),
            pltpu.SemaphoreType.DMA((2 * planes,)),
            pltpu.SemaphoreType.DMA((planes,)),
            pltpu.SemaphoreType.DMA((planes,)),
            pltpu.SemaphoreType.DMA((planes,)),
            pltpu.SemaphoreType.DMA((planes + 1,)),
        ],
        compiler_params=pltpu.CompilerParams(
            collective_id=0, has_side_effects=True, vmem_limit_bytes=VMEM_BYTES
        ),
        name="experts",
    )(normed, updated, gates_here, w_gate_up, w_down)


def gates_for_own(routes, route_weights, devices):
    gates = route_weights / jnp.sum(route_weights, axis=-1, keepdims=True)
    chosen = routes.T[None] == jnp.arange(devices, dtype=jnp.int32)[:, None, None]
    table = jnp.sum(jnp.where(chosen, gates.T[None], 0.0), axis=1)
    everyone = lax.all_gather(table, "ctx", axis=0)
    mine = lax.dynamic_index_in_dim(everyone, lax.axis_index("ctx"), axis=1, keepdims=False)
    return mine.reshape(devices // 2, 2 * routes.shape[0])


def fits(devices, rows, width, hidden):
    blocks = 3 * devices + 4
    return 2 * (blocks * rows * width + 3 * width * hidden) < VMEM_BYTES * 4 // 5


def local(
    residual,
    queries,
    keys,
    values,
    block_order,
    routes,
    route_weights,
    out_weight,
    norm_gain,
    w_gate_up,
    w_down,
):
    device_row_count = queries.shape[0]
    query_group_width = QUERY_HEADS // KEY_VALUE_HEADS
    devices = lax.axis_size("ctx")
    cycle_length = devices // SEQS
    own_index = lax.axis_index("ctx")
    full_weight = lax.all_gather(out_weight, "ctx", axis=1, tiled=True)
    gates_here = gates_for_own(routes, route_weights, devices)
    query_position = block_order[own_index]
    query_head_rows = (
        queries.reshape(device_row_count, KEY_VALUE_HEADS, query_group_width, HEAD_SIZE)
        .transpose(1, 2, 0, 3)
        .reshape(KEY_VALUE_HEADS, query_group_width * device_row_count, HEAD_SIZE)
    )
    query_offset = jnp.arange(query_group_width * device_row_count) % device_row_count
    key_offset = jnp.arange(device_row_count)
    scale = HEAD_SIZE ** (-0.5)

    def update(carry, key_value_tuple, key_position):
        summed, running_max, totals = carry
        local_key_block = key_value_tuple[0].reshape(device_row_count, KEY_VALUE_HEADS, HEAD_SIZE)
        local_value_block = key_value_tuple[1].reshape(device_row_count, KEY_VALUE_HEADS, HEAD_SIZE)
        scores = (
            jnp.einsum(
                "hqd,khd->hqk", query_head_rows, local_key_block, preferred_element_type=jnp.float32
            )
            * scale
        )
        visible = (
            key_position * device_row_count + key_offset[None, :]
            <= query_position * device_row_count + query_offset[:, None]
        )
        scores = jnp.where(visible[None], scores, -jnp.inf)
        new_max = jnp.maximum(running_max, jnp.max(scores, axis=-1))
        factor = jnp.exp(running_max - new_max)
        weights = jnp.exp(scores - new_max[..., None])
        totals = totals * factor + jnp.sum(weights, axis=-1)
        summed = summed * factor[..., None] + jnp.einsum(
            "hqk,khd->hqd",
            weights.astype(jnp.bfloat16),
            local_value_block,
            preferred_element_type=jnp.float32,
        )
        return (summed, new_max, totals)

    initial = (
        jnp.zeros((KEY_VALUE_HEADS, query_group_width * device_row_count, HEAD_SIZE), jnp.float32),
        jnp.full((KEY_VALUE_HEADS, query_group_width * device_row_count), -jnp.inf, jnp.float32),
        jnp.zeros((KEY_VALUE_HEADS, query_group_width * device_row_count), jnp.float32),
    )
    local_pair = jnp.stack([keys, values])
    carry = update(initial, local_pair, query_position)

    def advance(step, state):
        current, moving = state
        moving = shifted(moving, "ctx", SEQS)
        anchor = jnp.mod(own_index - SEQS * step, devices)
        key_position = block_order[anchor]
        current = lax.cond(
            key_position <= query_position,
            lambda inner: update(inner, moving, key_position),
            lambda inner: inner,
            current,
        )
        return (current, moving)

    carry, passed = lax.fori_loop(1, cycle_length, advance, (carry, local_pair))
    summed, running_max, totals = carry
    context = (
        (summed / totals[..., None])
        .reshape(KEY_VALUE_HEADS, query_group_width, device_row_count, HEAD_SIZE)
        .transpose(2, 0, 1, 3)
        .reshape(device_row_count, QUERY_HEADS * HEAD_SIZE)
        .astype(jnp.bfloat16)
    )
    projected = jnp.dot(context, full_weight, preferred_element_type=jnp.float32)
    updated = residual.astype(jnp.float32) + projected
    normed = (
        updated * lax.rsqrt(jnp.mean(updated * updated, axis=-1, keepdims=True) + 1e-06) * norm_gain
    ).astype(jnp.bfloat16)
    experts = devices * w_gate_up.shape[0]
    capacity = 9 * device_row_count * TOPK // (8 * experts)
    if fits(devices, device_row_count, D, FF):
        mixed = expert_call(normed, updated, gates_here, w_gate_up, w_down, capacity)
        return (context, mixed)
    expert_ids = routes.reshape(-1)
    one_hot = (expert_ids[:, None] == jnp.arange(experts, dtype=jnp.int32)[None, :]).astype(
        jnp.int32
    )
    ranks = jnp.sum(jnp.cumsum(one_hot, axis=0) * one_hot, axis=1) - 1
    target = expert_ids * capacity + ranks
    source_row = jnp.arange(device_row_count * TOPK) // TOPK
    outgoing = (
        jnp.zeros((experts * capacity, D), jnp.bfloat16)
        .at[target]
        .set(normed[source_row])
        .reshape(experts, capacity, D)
    )
    arrived = lax.all_to_all(outgoing, "ctx", split_axis=0, concat_axis=0, tiled=True)
    flat = arrived.reshape(-1, D)
    both = jnp.dot(flat, w_gate_up[0], preferred_element_type=jnp.float32)
    hidden = (jax.nn.silu(both[:, :FF]) * both[:, FF:]).astype(jnp.bfloat16)
    result = (
        jnp.dot(hidden, w_down[0], preferred_element_type=jnp.float32)
        .astype(jnp.bfloat16)
        .reshape(arrived.shape)
    )
    returned = lax.all_to_all(result, "ctx", split_axis=0, concat_axis=0, tiled=True)
    gathered = returned.reshape(-1, D)[target].reshape(device_row_count, TOPK, D)
    gates = route_weights / jnp.sum(route_weights, axis=-1, keepdims=True)
    mixed = updated
    for slot in range(TOPK):
        mixed = mixed + gates[:, slot : slot + 1] * gathered[:, slot].astype(jnp.float32)
    return (context, mixed.astype(jnp.bfloat16))


def solution(mesh):
    placed = (
        P(("groups", "ctx"), None),
        P(("groups", "ctx"), None),
        P(("groups", "ctx"), None),
        P(("groups", "ctx"), None),
        P("groups"),
        P(("groups", "ctx"), None),
        P(("groups", "ctx"), None),
        P(None, "ctx"),
        P(),
        P("ctx", None, None),
        P("ctx", None, None),
    )
    return jax.shard_map(
        local,
        mesh=mesh,
        in_specs=placed,
        out_specs=(P(("groups", "ctx"), None), P(("groups", "ctx"), None)),
        check_vma=False,
    )
```

```python
import functools

import jax
import jax.numpy as jnp
from jax import lax
from jax.experimental import pallas as pl
from jax.experimental.pallas import tpu as pltpu
from jax.sharding import PartitionSpec as P

D = 2048
HEAD_SIZE = 128
FF = 768
QUERY_HEADS = 16
KEY_VALUE_HEADS = 2
TOPK = 8
SEQS = 4


def shifted(array, axis, by):
    devices = lax.axis_size(axis)
    return lax.ppermute(array, axis, [(i, (i + by) % devices) for i in range(devices)])


VMEM_BYTES = 60 * 2**20
HALVES = 2


def put(src, dst, send_sem, recv_sem, to, axis="ctx"):
    return pltpu.make_async_remote_copy(
        src_ref=src,
        dst_ref=dst,
        send_sem=send_sem,
        recv_sem=recv_sem,
        device_id={axis: to},
        device_id_type=pl.DeviceIdType.MESH,
    )


def plane_at(step, z, planes):
    short = jnp.minimum(z, planes - 1 - z)
    sign = jnp.where(2 * z < planes - 1, 1, -1)
    near = (step + 1) // 2 * (2 * (step % 2) - 1)
    return z + sign * jnp.where(step <= 2 * short, near, step - short)


def layer_kernel(
    planes,
    cap,
    order_ref,
    residual_ref,
    queries_ref,
    keys_ref,
    values_ref,
    table_ref,
    gain_ref,
    weight_ref,
    up_hbm,
    down_hbm,
    context_ref,
    out_ref,
    kv,
    tables,
    gates_ref,
    columns,
    updated_ref,
    rows_all,
    contrib,
    from_core,
    from_y,
    from_z,
    w_up,
    w_down,
    ranks,
    picked,
    act,
    kv_s,
    kv_r,
    t_s,
    t_r,
    o_recv,
    o_up_s,
    o_dn_s,
    o_y_s,
    o_x_s,
    o_c_s,
    w_sem,
    recv,
    up_s,
    dn_s,
    y_s,
    c_s,
    rc_s,
    rc_r,
    ry_s,
    ry_r,
    rz_s,
    rz_r,
):
    n, width = residual_ref.shape
    hidden = w_down.shape[0]
    pair = 2 * n
    me = lax.axis_index("ctx")
    z, place = me // SEQS, me % SEQS
    y, c = place // 2, place % 2
    at_y = z * SEQS + (1 - y) * 2 + c
    at_core = z * SEQS + y * 2 + (1 - c)
    above, below = z < planes - 1, z > 0

    def block(ref, index):
        return ref.at[pl.ds(pl.multiple_of(index * n, n), n)]

    load_up = pltpu.make_async_copy(up_hbm.at[0], w_up, w_sem.at[0])
    load_down = pltpu.make_async_copy(down_hbm.at[0], w_down, w_sem.at[1])
    load_up.start()
    load_down.start()

    barrier = pltpu.get_barrier_semaphore()

    def greet(to, axis="ctx"):
        pl.semaphore_signal(
            barrier, inc=1, device_id={axis: to}, device_id_type=pl.DeviceIdType.MESH
        )

    group = lax.axis_index("groups")
    at_x = 1 - group
    experts = planes * SEQS
    greet(at_x, "groups")
    greet(at_y)
    greet(at_core)
    for by in range(1, planes):
        greet(lax.rem(z + by, planes) * SEQS + place)
    kv_width = keys_ref.shape[1]
    own_kv = block(kv, z)
    own_kv[:, :kv_width] = keys_ref[...]
    own_kv[:, kv_width:] = values_ref[...]
    column = c * 2 + y

    def table(col, plane, count):
        start = pl.multiple_of((col * planes + plane) * experts, experts)
        return tables.at[pl.ds(start, count * experts)]

    table(column, z, 1)[...] = table_ref[...]
    columns[me] = weight_ref[...]
    pl.semaphore_wait(barrier, planes + 2)

    def kv_copy(plane, by):
        return put(block(kv, plane), block(kv, plane), kv_s.at[by], kv_r.at[plane], at_y)

    def send_kv(by):
        to = lax.rem(z + by, planes) * SEQS + place
        return (
            put(own_kv, own_kv, kv_s.at[by], kv_r.at[z], to),
            put(table(column, z, 1), table(column, z, 1), t_s.at[by], t_r.at[z], to),
        )

    def tables_to_y():
        part = table(column, 0, planes)
        return put(part, part, t_s.at[planes], t_r.at[planes], at_y)

    def tables_to_core():
        part = table(c * 2, 0, 2 * planes)
        return put(part, part, t_s.at[planes + 1], t_r.at[planes + 1], at_core)

    for by in range(1, planes):
        for copy in send_kv(by):
            copy.start()

    def column_copy(index, sem, to, axis="ctx"):
        return put(columns.at[index], columns.at[index], sem, o_recv.at[index], to, axis)

    def column_forwards(p):
        index = p * SEQS + place
        return (
            (above & (p <= z), column_copy(index, o_up_s.at[p], me + SEQS)),
            (below & (p >= z), column_copy(index, o_dn_s.at[p], me - SEQS)),
            (c == group, column_copy(index, o_y_s.at[p], at_y)),
            (None, column_copy(index, o_c_s.at[p * 2 + y], at_core)),
        )

    def column_seconds(p):
        index = p * SEQS + (1 - y) * 2 + c
        return (
            (c == group, column_copy(index, o_x_s.at[p], at_x, "groups")),
            (None, column_copy(index, o_c_s.at[p * 2 + 1 - y], at_core)),
        )

    def start_all(copies):
        for condition, copy in copies:
            if condition is None:
                copy.start()
            else:
                pl.when(condition)(copy.start)

    def sent_all(copies):
        for condition, copy in copies:
            if condition is None:
                copy.wait_send()
            else:
                pl.when(condition)(copy.wait_send)

    start_all(column_forwards(z))
    for by in range(1, planes):
        plane = lax.rem(z + by, planes)
        kv_copy(plane, by).wait_recv()
        put(
            table(column, plane, 1), table(column, plane, 1), t_s.at[by], t_r.at[plane], at_y
        ).wait_recv()
    tables_to_y().start()

    total_keys = planes * n
    lane = lax.broadcasted_iota(jnp.int32, (n, total_keys), 1)
    key_plane = lane // n
    key_position = lane % n
    for plane in range(planes):
        key_position = key_position + jnp.where(
            key_plane == plane, order_ref[plane * SEQS + place] * n, 0
        )
    query_position = order_ref[me] * n + lax.broadcasted_iota(jnp.int32, (n, total_keys), 0)
    visible = key_position <= query_position
    heads = width // HEAD_SIZE
    kv_heads = kv_width // HEAD_SIZE

    def attend(head, carry):
        cols = pl.ds(pl.multiple_of(head * HEAD_SIZE, HEAD_SIZE), HEAD_SIZE)
        kv_head = head // (heads // kv_heads)
        key_cols = pl.ds(pl.multiple_of(kv_head * HEAD_SIZE, HEAD_SIZE), HEAD_SIZE)
        value_cols = pl.ds(pl.multiple_of(kv_width + kv_head * HEAD_SIZE, HEAD_SIZE), HEAD_SIZE)
        scores = lax.dot_general(
            queries_ref[:, cols],
            kv[:, key_cols],
            (((1,), (1,)), ((), ())),
            preferred_element_type=jnp.float32,
        ) * (HEAD_SIZE**-0.5)
        scores = jnp.where(visible, scores, -jnp.inf)
        weights = jnp.exp(scores - jnp.max(scores, axis=1, keepdims=True))
        total = jnp.sum(weights, axis=1, keepdims=True)
        summed = jnp.dot(
            weights.astype(jnp.bfloat16), kv[:, value_cols], preferred_element_type=jnp.float32
        )
        context_ref[:, cols] = (summed / total).astype(jnp.bfloat16)
        return carry

    lax.fori_loop(0, heads, attend, 0, unroll=4)
    tables_to_y().wait_recv()
    tables_to_core().start()

    def weight_step(k, carry):
        @pl.when(k < planes)
        def _():
            p = plane_at(k, z, planes)
            column_copy(p * SEQS + place, o_y_s.at[p], at_y).wait_recv()
            start_all(column_forwards(p))

        p = plane_at(k - 1, z, planes)
        column_copy(p * SEQS + (1 - y) * 2 + c, o_y_s.at[p], at_y).wait_recv()
        start_all(column_seconds(p))
        for row in range(2):
            column_copy(p * SEQS + row * 2 + 1 - c, o_y_s.at[p], at_core).wait_recv()
        for spot in range(SEQS):
            index = p * SEQS + spot
            each = columns.shape[2]
            cols = pl.ds(pl.multiple_of(index * each, each), each)
            updated_ref[:, cols] = residual_ref[:, cols].astype(jnp.float32) + jnp.dot(
                context_ref[...], columns[index], preferred_element_type=jnp.float32
            )
        return carry

    lax.fori_loop(1, planes + 1, weight_step, 0)
    tables_to_core().wait_recv()

    def norm(i, carry):
        rows = pl.ds(pl.multiple_of(i * 16, 16), 16)
        rows_there = pl.ds(pl.multiple_of(me * n + i * 16, 16), 16)
        updated = updated_ref[rows, :]
        mean = jnp.mean(updated * updated, axis=1, keepdims=True)
        rows_all[rows_there, :] = (updated * lax.rsqrt(mean + 1e-06) * gain_ref[...]).astype(
            jnp.bfloat16
        )
        return carry

    lax.fori_loop(0, n // 16, norm, 0)
    for p in range(planes):
        for row in range(2):
            for core in range(2):
                at = ((core * 2 + row) * planes + p) * experts + me
                gates_ref[pl.ds(p * 2 + row, 1), pl.ds(core * n, n)] = tables[pl.ds(at, 1), :]

    def gather_copy(index, sem, to):
        return put(block(rows_all, index), block(rows_all, index), sem, recv.at[index], to)

    def forwards(p):
        index = p * SEQS + place
        return (
            (above & (p <= z), gather_copy(index, up_s.at[p], me + SEQS)),
            (below & (p >= z), gather_copy(index, dn_s.at[p], me - SEQS)),
            (None, gather_copy(index, y_s.at[p], at_y)),
            (None, gather_copy(index, c_s.at[p * 2 + y], at_core)),
        )

    def second_forward(p):
        return gather_copy(p * SEQS + (1 - y) * 2 + c, c_s.at[p * 2 + 1 - y], at_core)

    def core_return(p, row):
        return put(
            block(contrib, p * SEQS + row * 2 + 1 - c),
            block(from_core, p * 2 + row),
            rc_s.at[p * 2 + row],
            rc_r.at[p * 2 + row],
            at_core,
        )

    small = n // HALVES

    def piece(ref, index, h):
        return ref.at[pl.ds(pl.multiple_of(index * n + h * small, small), small)]

    def y_return(p, h):
        at = p * HALVES + h
        return put(
            piece(contrib, p * SEQS + (1 - y) * 2 + c, h),
            piece(from_y, p, h),
            ry_s.at[at],
            ry_r.at[at],
            at_y,
        )

    def z_return(p, slot, h, to):
        return put(
            piece(contrib, p * SEQS + place, h),
            piece(from_z, slot, h),
            rz_s.at[p * HALVES + h],
            rz_r.at[slot * HALVES + h],
            to,
        )

    shape = (pair, pair)
    earlier = lax.broadcasted_iota(jnp.int32, shape, 0)
    later = lax.broadcasted_iota(jnp.int32, shape, 1)
    before = (earlier < later) & (earlier // n == later // n)
    routed = gates_ref[...] > 0
    count = jnp.dot(
        routed.astype(jnp.bfloat16), before.astype(jnp.bfloat16), preferred_element_type=jnp.float32
    ).astype(jnp.int32)
    offset = lax.broadcasted_iota(jnp.int32, count.shape, 1) // n * cap
    ranks[...] = jnp.where(routed, count + offset, -1)

    def compute(p):
        parts = []
        for half in range(2):
            row = pl.ds(p * 2 + half, 1)
            hit = lax.broadcasted_iota(jnp.int32, (2 * cap, pair), 0) == ranks[row, :]
            gate = jnp.sum(jnp.where(hit, gates_ref[row, :], 0.0), axis=1, keepdims=True)
            choose = hit.astype(jnp.float32).astype(jnp.bfloat16)
            parts.append((choose, gate))
        tile = 512

        def pick(j, carry):
            cols = pl.ds(pl.multiple_of(j * tile, tile), tile)
            for half in range(2):
                source = pl.ds(pl.multiple_of((p * 2 + half) * pair, pair), pair)
                picked[pl.ds(half * 2 * cap, 2 * cap), cols] = jnp.dot(
                    parts[half][0], rows_all[source, cols], preferred_element_type=jnp.float32
                ).astype(jnp.bfloat16)
            return carry

        lax.fori_loop(0, width // tile, pick, 0)
        narrow = 256

        def gate_up(j, carry):
            first = pl.ds(pl.multiple_of(j * narrow, narrow), narrow)
            second = pl.ds(pl.multiple_of(hidden + j * narrow, narrow), narrow)
            v = jnp.dot(picked[...], w_up[:, first], preferred_element_type=jnp.float32)
            u = jnp.dot(picked[...], w_up[:, second], preferred_element_type=jnp.float32)
            act[:, first] = (v / (1.0 + jnp.exp(-v)) * u).astype(jnp.bfloat16)
            return carry

        lax.fori_loop(0, hidden // narrow, gate_up, 0)

        def down(j, carry):
            cols = pl.ds(pl.multiple_of(j * tile, tile), tile)
            for half in range(2):
                choose, gate = parts[half]
                source = pl.ds(pl.multiple_of((p * 2 + half) * pair, pair), pair)
                result = jnp.dot(
                    act[pl.ds(half * 2 * cap, 2 * cap), :],
                    w_down[:, cols],
                    preferred_element_type=jnp.float32,
                )
                contrib[source, cols] = lax.dot_general(
                    choose,
                    (result * gate).astype(jnp.bfloat16),
                    (((0,), (0,)), ((), ())),
                    preferred_element_type=jnp.float32,
                ).astype(jnp.bfloat16)
            return carry

        lax.fori_loop(0, width // tile, down, 0)

    def advance(k, carry):
        @pl.when(k < planes)
        def _():
            p = plane_at(k, z, planes)

            @pl.when(k > 0)
            def _():
                gather_copy(p * SEQS + place, y_s.at[p], at_y).wait_recv()

            start_all(forwards(p))

        @pl.when(k > 0)
        def _():
            p = plane_at(k - 1, z, planes)
            second_forward(p).wait_recv()
            second_forward(p).start()
            for row in range(2):
                gather_copy(p * SEQS + row * 2 + 1 - c, c_s.at[0], at_core).wait_recv()

            @pl.when(k == 1)
            def _():
                load_up.wait()
                load_down.wait()

            compute(p)
            for row in range(2):
                core_return(p, row).start()

        return carry

    lax.fori_loop(0, planes + 1, advance, 0)
    chunk = 16

    def add_up(target, terms):
        def some(i, carry):
            here = pl.ds(pl.multiple_of(i * chunk, chunk), chunk)
            total = terms[0][here, :].astype(jnp.float32)
            for term in terms[1:]:
                total = total + term[here, :].astype(jnp.float32)
            target[here, :] = total.astype(target.dtype)
            return carry

        lax.fori_loop(0, small // chunk, some, 0)

    def core_sum(i, carry):
        p = plane_at(planes - 1 - i, z, planes)
        for row in range(2):
            core_return(p, row).wait_recv()
        for h in range(HALVES):
            other = piece(contrib, p * SEQS + (1 - y) * 2 + c, h)
            add_up(other, [other, piece(from_core, p * 2 + 1 - y, h)])
            y_return(p, h).start()
        return carry

    lax.fori_loop(0, planes, core_sum, 0)

    def chain(i, carry):
        p = plane_at(planes - 1 - i // HALVES, z, planes)
        h = i % HALVES
        y_return(p, h).wait_recv()
        own = piece(contrib, p * SEQS + place, h)
        terms = [own, piece(from_core, p * 2 + y, h), piece(from_y, p, h)]
        onward = ((p < z) & above) | ((p > z) & below)

        @pl.when(onward)
        def _():
            z_return(p, p, h, at_y).wait_recv()
            add_up(own, terms + [piece(from_z, p, h)])

        pl.when(jnp.logical_not(onward))(lambda: add_up(own, terms))

        @pl.when(p < z)
        def _():
            z_return(p, jnp.where(p == z - 1, planes, p), h, me - SEQS).start()

        @pl.when(p > z)
        def _():
            z_return(p, p, h, me + SEQS).start()

        return carry

    lax.fori_loop(0, (planes - 1) * HALVES, chain, 0)

    def last(h, carry):
        y_return(z, h).wait_recv()
        result = piece(out_ref, 0, h)
        terms = [
            piece(updated_ref, 0, h),
            piece(contrib, me, h),
            piece(from_core, z * 2 + y, h),
            piece(from_y, z, h),
        ]
        low, high = piece(from_z, z, h), piece(from_z, planes, h)
        pl.when(below)(lambda: z_return(z, z, h, at_y).wait_recv())
        pl.when(above)(lambda: z_return(z, planes, h, at_y).wait_recv())
        pl.when(below & above)(lambda: add_up(result, terms + [low, high]))
        pl.when(below & jnp.logical_not(above))(lambda: add_up(result, terms + [low]))
        pl.when(jnp.logical_not(below) & above)(lambda: add_up(result, terms + [high]))
        return carry

    lax.fori_loop(0, HALVES, last, 0)

    for by in range(1, planes):
        for copy in send_kv(by):
            copy.wait_send()
    tables_to_y().wait_send()
    tables_to_core().wait_send()

    def finish(p, carry):
        sent_all(column_forwards(p))
        sent_all(column_seconds(p))
        sent_all(forwards(p))
        second_forward(p).wait_send()
        for row in range(2):
            core_return(p, row).wait_send()
        for h in range(HALVES):
            y_return(p, h).wait_send()

        @pl.when(p != z)
        def _():
            for h in range(HALVES):
                z_return(p, p, h, at_y).wait_send()

        return carry

    lax.fori_loop(0, planes, finish, 0)


def layer_call(
    order, residual, queries, keys, values, table, gain, out_weight, w_gate_up, w_down, cap
):
    n, width = residual.shape
    hidden = w_down.shape[1]
    devices = lax.axis_size("ctx")
    planes = devices // SEQS
    vmem = pl.BlockSpec(memory_space=pltpu.VMEM)
    anywhere = pl.BlockSpec(memory_space=pl.ANY)
    bf16 = jnp.bfloat16
    dma = pltpu.SemaphoreType.DMA
    return pl.pallas_call(
        functools.partial(layer_kernel, planes, cap),
        out_shape=[jax.ShapeDtypeStruct((n, width), bf16)] * 2,
        in_specs=[pl.BlockSpec(memory_space=pltpu.SMEM)] + [vmem] * 7 + [anywhere] * 2,
        out_specs=[vmem, vmem],
        scratch_shapes=[
            pltpu.VMEM((planes * n, 2 * keys.shape[1]), bf16),
            pltpu.VMEM((devices * devices, n), jnp.float32),
            pltpu.VMEM((2 * planes, 2 * n), jnp.float32),
            pltpu.VMEM((devices,) + out_weight.shape, bf16),
            pltpu.VMEM((n, width), jnp.float32),
            pltpu.VMEM((devices * n, width), bf16),
            pltpu.VMEM((devices * n, width), bf16),
            pltpu.VMEM((2 * planes * n, width), bf16),
            pltpu.VMEM((planes * n, width), bf16),
            pltpu.VMEM(((planes + 1) * n, width), bf16),
            pltpu.VMEM(w_gate_up.shape[1:], bf16),
            pltpu.VMEM(w_down.shape[1:], bf16),
            pltpu.VMEM((2 * planes, 2 * n), jnp.int32),
            pltpu.VMEM((SEQS * cap, width), bf16),
            pltpu.VMEM((SEQS * cap, hidden), bf16),
            dma((planes,)),
            dma((planes,)),
            dma((planes + 2,)),
            dma((planes + 2,)),
            dma((devices,)),
            dma((planes,)),
            dma((planes,)),
            dma((planes,)),
            dma((planes,)),
            dma((2 * planes,)),
            dma((2,)),
            dma((devices,)),
            dma((planes,)),
            dma((planes,)),
            dma((planes,)),
            dma((2 * planes,)),
            dma((2 * planes,)),
            dma((2 * planes,)),
            dma((HALVES * planes,)),
            dma((HALVES * planes,)),
            dma((HALVES * planes,)),
            dma((HALVES * (planes + 1),)),
        ],
        compiler_params=pltpu.CompilerParams(
            collective_id=0, has_side_effects=True, vmem_limit_bytes=VMEM_BYTES
        ),
        name="layer",
    )(order, residual, queries, keys, values, table, gain, out_weight, w_gate_up, w_down)


def gate_table(routes, route_weights, experts):
    gates = route_weights / jnp.sum(route_weights, axis=-1, keepdims=True)
    chosen = routes.T[None] == jnp.arange(experts, dtype=jnp.int32)[:, None, None]
    return jnp.sum(jnp.where(chosen, gates.T[None], 0.0), axis=1)


def fits(devices, rows, width, hidden):
    blocks = 4 * devices + 8
    return lax.axis_size("groups") == 2 and 2 * (blocks * rows * width + 3 * width * hidden) < VMEM_BYTES * 4 // 5


def local(
    residual,
    queries,
    keys,
    values,
    block_order,
    routes,
    route_weights,
    out_weight,
    norm_gain,
    w_gate_up,
    w_down,
):
    device_row_count = queries.shape[0]
    query_group_width = QUERY_HEADS // KEY_VALUE_HEADS
    devices = lax.axis_size("ctx")
    cycle_length = devices // SEQS
    own_index = lax.axis_index("ctx")
    experts = devices * w_gate_up.shape[0]
    capacity = 9 * device_row_count * TOPK // (8 * experts)
    if fits(devices, device_row_count, D, FF):
        return tuple(
            layer_call(
                block_order,
                residual,
                queries,
                keys,
                values,
                gate_table(routes, route_weights, experts),
                norm_gain.reshape(1, -1),
                out_weight,
                w_gate_up,
                w_down,
                capacity,
            )
        )
    full_weight = lax.all_gather(out_weight, "ctx", axis=1, tiled=True)
    query_position = block_order[own_index]
    query_head_rows = (
        queries.reshape(device_row_count, KEY_VALUE_HEADS, query_group_width, HEAD_SIZE)
        .transpose(1, 2, 0, 3)
        .reshape(KEY_VALUE_HEADS, query_group_width * device_row_count, HEAD_SIZE)
    )
    query_offset = jnp.arange(query_group_width * device_row_count) % device_row_count
    key_offset = jnp.arange(device_row_count)
    scale = HEAD_SIZE ** (-0.5)

    def update(carry, key_value_tuple, key_position):
        summed, running_max, totals = carry
        local_key_block = key_value_tuple[0].reshape(device_row_count, KEY_VALUE_HEADS, HEAD_SIZE)
        local_value_block = key_value_tuple[1].reshape(device_row_count, KEY_VALUE_HEADS, HEAD_SIZE)
        scores = (
            jnp.einsum(
                "hqd,khd->hqk", query_head_rows, local_key_block, preferred_element_type=jnp.float32
            )
            * scale
        )
        visible = (
            key_position * device_row_count + key_offset[None, :]
            <= query_position * device_row_count + query_offset[:, None]
        )
        scores = jnp.where(visible[None], scores, -jnp.inf)
        new_max = jnp.maximum(running_max, jnp.max(scores, axis=-1))
        factor = jnp.exp(running_max - new_max)
        weights = jnp.exp(scores - new_max[..., None])
        totals = totals * factor + jnp.sum(weights, axis=-1)
        summed = summed * factor[..., None] + jnp.einsum(
            "hqk,khd->hqd",
            weights.astype(jnp.bfloat16),
            local_value_block,
            preferred_element_type=jnp.float32,
        )
        return (summed, new_max, totals)

    initial = (
        jnp.zeros((KEY_VALUE_HEADS, query_group_width * device_row_count, HEAD_SIZE), jnp.float32),
        jnp.full((KEY_VALUE_HEADS, query_group_width * device_row_count), -jnp.inf, jnp.float32),
        jnp.zeros((KEY_VALUE_HEADS, query_group_width * device_row_count), jnp.float32),
    )
    local_pair = jnp.stack([keys, values])
    carry = update(initial, local_pair, query_position)

    def advance(step, state):
        current, moving = state
        moving = shifted(moving, "ctx", SEQS)
        anchor = jnp.mod(own_index - SEQS * step, devices)
        key_position = block_order[anchor]
        current = lax.cond(
            key_position <= query_position,
            lambda inner: update(inner, moving, key_position),
            lambda inner: inner,
            current,
        )
        return (current, moving)

    carry, passed = lax.fori_loop(1, cycle_length, advance, (carry, local_pair))
    summed, running_max, totals = carry
    context = (
        (summed / totals[..., None])
        .reshape(KEY_VALUE_HEADS, query_group_width, device_row_count, HEAD_SIZE)
        .transpose(2, 0, 1, 3)
        .reshape(device_row_count, QUERY_HEADS * HEAD_SIZE)
        .astype(jnp.bfloat16)
    )
    projected = jnp.dot(context, full_weight, preferred_element_type=jnp.float32)
    updated = residual.astype(jnp.float32) + projected
    normed = (
        updated * lax.rsqrt(jnp.mean(updated * updated, axis=-1, keepdims=True) + 1e-06) * norm_gain
    ).astype(jnp.bfloat16)
    experts = devices * w_gate_up.shape[0]
    capacity = 9 * device_row_count * TOPK // (8 * experts)
    expert_ids = routes.reshape(-1)
    one_hot = (expert_ids[:, None] == jnp.arange(experts, dtype=jnp.int32)[None, :]).astype(
        jnp.int32
    )
    ranks = jnp.sum(jnp.cumsum(one_hot, axis=0) * one_hot, axis=1) - 1
    target = expert_ids * capacity + ranks
    source_row = jnp.arange(device_row_count * TOPK) // TOPK
    outgoing = (
        jnp.zeros((experts * capacity, D), jnp.bfloat16)
        .at[target]
        .set(normed[source_row])
        .reshape(experts, capacity, D)
    )
    arrived = lax.all_to_all(outgoing, "ctx", split_axis=0, concat_axis=0, tiled=True)
    flat = arrived.reshape(-1, D)
    both = jnp.dot(flat, w_gate_up[0], preferred_element_type=jnp.float32)
    hidden = (jax.nn.silu(both[:, :FF]) * both[:, FF:]).astype(jnp.bfloat16)
    result = (
        jnp.dot(hidden, w_down[0], preferred_element_type=jnp.float32)
        .astype(jnp.bfloat16)
        .reshape(arrived.shape)
    )
    returned = lax.all_to_all(result, "ctx", split_axis=0, concat_axis=0, tiled=True)
    gathered = returned.reshape(-1, D)[target].reshape(device_row_count, TOPK, D)
    gates = route_weights / jnp.sum(route_weights, axis=-1, keepdims=True)
    mixed = updated
    for slot in range(TOPK):
        mixed = mixed + gates[:, slot : slot + 1] * gathered[:, slot].astype(jnp.float32)
    return (context, mixed.astype(jnp.bfloat16))


def solution(mesh):
    placed = (
        P(("groups", "ctx"), None),
        P(("groups", "ctx"), None),
        P(("groups", "ctx"), None),
        P(("groups", "ctx"), None),
        P("groups"),
        P(("groups", "ctx"), None),
        P(("groups", "ctx"), None),
        P(None, "ctx"),
        P(),
        P("ctx", None, None),
        P("ctx", None, None),
    )
    return jax.shard_map(
        local,
        mesh=mesh,
        in_specs=placed,
        out_specs=(P(("groups", "ctx"), None), P(("groups", "ctx"), None)),
        check_vma=False,
    )
```

```python
import functools

import jax
import jax.numpy as jnp
from jax import lax
from jax.experimental import pallas as pl
from jax.experimental.pallas import tpu as pltpu
from jax.sharding import PartitionSpec as P

D = 2048
HEAD_SIZE = 128
FF = 768
QUERY_HEADS = 16
KEY_VALUE_HEADS = 2
TOPK = 8
SEQS = 4


def shifted(array, axis, by):
    devices = lax.axis_size(axis)
    return lax.ppermute(array, axis, [(i, (i + by) % devices) for i in range(devices)])


VMEM_BYTES = 60 * 2**20
HALVES = 2


def put(src, dst, send_sem, recv_sem, to, axis="ctx"):
    return pltpu.make_async_remote_copy(
        src_ref=src,
        dst_ref=dst,
        send_sem=send_sem,
        recv_sem=recv_sem,
        device_id={axis: to},
        device_id_type=pl.DeviceIdType.MESH,
    )


def plane_at(step, z, planes):
    short = jnp.minimum(z, planes - 1 - z)
    sign = jnp.where(2 * z < planes - 1, 1, -1)
    near = (step + 1) // 2 * (2 * (step % 2) - 1)
    return z + sign * jnp.where(step <= 2 * short, near, step - short)


def layer_kernel(
    planes,
    cap,
    order_ref,
    residual_ref,
    queries_ref,
    keys_ref,
    values_ref,
    table_ref,
    gain_ref,
    weight_ref,
    up_hbm,
    down_hbm,
    context_ref,
    out_ref,
    kv,
    tables,
    gates_ref,
    columns,
    updated_ref,
    rows_all,
    contrib,
    from_core,
    from_y,
    from_z,
    w_up,
    w_down,
    ranks,
    picked,
    act,
    kv_s,
    kv_r,
    t_s,
    t_r,
    o_recv,
    o_up_s,
    o_dn_s,
    o_y_s,
    o_x_s,
    o_c_s,
    w_sem,
    recv,
    up_s,
    dn_s,
    y_s,
    c_s,
    rc_s,
    rc_r,
    ry_s,
    ry_r,
    rz_s,
    rz_r,
):
    n, width = residual_ref.shape
    hidden = w_down.shape[0]
    pair = 2 * n
    me = lax.axis_index("ctx")
    z, place = me // SEQS, me % SEQS
    y, c = place // 2, place % 2
    at_y = z * SEQS + (1 - y) * 2 + c
    at_core = z * SEQS + y * 2 + (1 - c)
    above, below = z < planes - 1, z > 0

    def block(ref, index):
        return ref.at[pl.ds(pl.multiple_of(index * n, n), n)]

    load_up = pltpu.make_async_copy(up_hbm.at[0], w_up, w_sem.at[0])
    load_down = pltpu.make_async_copy(down_hbm.at[0], w_down, w_sem.at[1])
    load_up.start()
    load_down.start()

    barrier = pltpu.get_barrier_semaphore()

    def greet(to, axis="ctx"):
        pl.semaphore_signal(
            barrier, inc=1, device_id={axis: to}, device_id_type=pl.DeviceIdType.MESH
        )

    group = lax.axis_index("groups")
    at_x = 1 - group
    experts = planes * SEQS
    greet(at_x, "groups")
    greet(at_y)
    greet(at_core)
    for by in range(1, planes):
        greet(lax.rem(z + by, planes) * SEQS + place)
    kv_width = keys_ref.shape[1]
    own_kv = block(kv, z)
    own_kv[:, :kv_width] = keys_ref[...]
    own_kv[:, kv_width:] = values_ref[...]
    column = c * 2 + y

    def table(col, plane, count):
        start = pl.multiple_of((col * planes + plane) * experts, experts)
        return tables.at[pl.ds(start, count * experts)]

    table(column, z, 1)[...] = table_ref[...]
    columns[me] = weight_ref[...]
    pl.semaphore_wait(barrier, planes + 2)

    def kv_copy(plane, by):
        return put(block(kv, plane), block(kv, plane), kv_s.at[by], kv_r.at[plane], at_y)

    def send_kv(by):
        to = lax.rem(z + by, planes) * SEQS + place
        return (
            put(own_kv, own_kv, kv_s.at[by], kv_r.at[z], to),
            put(table(column, z, 1), table(column, z, 1), t_s.at[by], t_r.at[z], to),
        )

    def tables_to_y():
        part = table(column, 0, planes)
        return put(part, part, t_s.at[planes], t_r.at[planes], at_y)

    def tables_to_core():
        part = table(c * 2, 0, 2 * planes)
        return put(part, part, t_s.at[planes + 1], t_r.at[planes + 1], at_core)

    for by in range(1, planes):
        for copy in send_kv(by):
            copy.start()

    def column_copy(index, sem, to, axis="ctx"):
        return put(columns.at[index], columns.at[index], sem, o_recv.at[index], to, axis)

    def column_forwards(p):
        index = p * SEQS + place
        return (
            (above & (p <= z), column_copy(index, o_up_s.at[p], me + SEQS)),
            (below & (p >= z), column_copy(index, o_dn_s.at[p], me - SEQS)),
            (c == group, column_copy(index, o_y_s.at[p], at_y)),
            (None, column_copy(index, o_c_s.at[p * 2 + y], at_core)),
        )

    def column_seconds(p):
        index = p * SEQS + (1 - y) * 2 + c
        return (
            column_copy(index, o_x_s.at[p], at_x, "groups"),
            column_copy(index, o_c_s.at[p * 2 + 1 - y], at_core),
        )

    def start_all(copies):
        for condition, copy in copies:
            if condition is None:
                copy.start()
            else:
                pl.when(condition)(copy.start)

    def sent_all(copies):
        for condition, copy in copies:
            if condition is None:
                copy.wait_send()
            else:
                pl.when(condition)(copy.wait_send)

    start_all(column_forwards(z))
    for by in range(1, planes):
        plane = lax.rem(z + by, planes)
        kv_copy(plane, by).wait_recv()
        put(
            table(column, plane, 1), table(column, plane, 1), t_s.at[by], t_r.at[plane], at_y
        ).wait_recv()
    tables_to_y().start()

    total_keys = planes * n
    lane = lax.broadcasted_iota(jnp.int32, (n, total_keys), 1)
    key_plane = lane // n
    key_position = lane % n
    for plane in range(planes):
        key_position = key_position + jnp.where(
            key_plane == plane, order_ref[plane * SEQS + place] * n, 0
        )
    query_position = order_ref[me] * n + lax.broadcasted_iota(jnp.int32, (n, total_keys), 0)
    visible = key_position <= query_position
    heads = width // HEAD_SIZE
    kv_heads = kv_width // HEAD_SIZE

    def attend(head, carry):
        cols = pl.ds(pl.multiple_of(head * HEAD_SIZE, HEAD_SIZE), HEAD_SIZE)
        kv_head = head // (heads // kv_heads)
        key_cols = pl.ds(pl.multiple_of(kv_head * HEAD_SIZE, HEAD_SIZE), HEAD_SIZE)
        value_cols = pl.ds(pl.multiple_of(kv_width + kv_head * HEAD_SIZE, HEAD_SIZE), HEAD_SIZE)
        scores = lax.dot_general(
            queries_ref[:, cols],
            kv[:, key_cols],
            (((1,), (1,)), ((), ())),
            preferred_element_type=jnp.float32,
        ) * (HEAD_SIZE**-0.5)
        scores = jnp.where(visible, scores, -jnp.inf)
        weights = jnp.exp(scores - jnp.max(scores, axis=1, keepdims=True))
        total = jnp.sum(weights, axis=1, keepdims=True)
        summed = jnp.dot(
            weights.astype(jnp.bfloat16), kv[:, value_cols], preferred_element_type=jnp.float32
        )
        context_ref[:, cols] = (summed / total).astype(jnp.bfloat16)
        return carry

    lax.fori_loop(0, heads, attend, 0, unroll=4)
    tables_to_y().wait_recv()
    tables_to_core().start()

    def weight_step(k, carry):
        @pl.when(k < planes)
        def _():
            p = plane_at(k, z, planes)
            column_copy(p * SEQS + place, o_y_s.at[p], at_y).wait_recv()
            start_all(column_forwards(p))

        @pl.when((k <= planes) & (c == group))
        def _():
            p = plane_at(k - 1, z, planes)
            column_copy(p * SEQS + (1 - y) * 2 + c, o_y_s.at[p], at_y).wait_recv()
            for copy in column_seconds(p):
                copy.start()

        @pl.when(k > 1)
        def _():
            p = plane_at(k - 2, z, planes)

            @pl.when(c != group)
            def _():
                column_copy(p * SEQS + (1 - y) * 2 + c, o_y_s.at[p], at_y).wait_recv()
                column_seconds(p)[1].start()

            for row in range(2):
                column_copy(p * SEQS + row * 2 + 1 - c, o_y_s.at[p], at_core).wait_recv()
            for spot in range(SEQS):
                index = p * SEQS + spot
                each = columns.shape[2]
                cols = pl.ds(pl.multiple_of(index * each, each), each)
                updated_ref[:, cols] = residual_ref[:, cols].astype(jnp.float32) + jnp.dot(
                    context_ref[...], columns[index], preferred_element_type=jnp.float32
                )

        return carry

    lax.fori_loop(1, planes + 2, weight_step, 0)
    tables_to_core().wait_recv()

    def norm(i, carry):
        rows = pl.ds(pl.multiple_of(i * 16, 16), 16)
        rows_there = pl.ds(pl.multiple_of(me * n + i * 16, 16), 16)
        updated = updated_ref[rows, :]
        mean = jnp.mean(updated * updated, axis=1, keepdims=True)
        rows_all[rows_there, :] = (updated * lax.rsqrt(mean + 1e-06) * gain_ref[...]).astype(
            jnp.bfloat16
        )
        return carry

    lax.fori_loop(0, n // 16, norm, 0)
    for p in range(planes):
        for row in range(2):
            for core in range(2):
                at = ((core * 2 + row) * planes + p) * experts + me
                gates_ref[pl.ds(p * 2 + row, 1), pl.ds(core * n, n)] = tables[pl.ds(at, 1), :]

    def gather_copy(index, sem, to):
        return put(block(rows_all, index), block(rows_all, index), sem, recv.at[index], to)

    def forwards(p):
        index = p * SEQS + place
        return (
            (above & (p <= z), gather_copy(index, up_s.at[p], me + SEQS)),
            (below & (p >= z), gather_copy(index, dn_s.at[p], me - SEQS)),
            (None, gather_copy(index, y_s.at[p], at_y)),
            (None, gather_copy(index, c_s.at[p * 2 + y], at_core)),
        )

    def second_forward(p):
        return gather_copy(p * SEQS + (1 - y) * 2 + c, c_s.at[p * 2 + 1 - y], at_core)

    def core_return(p, row):
        return put(
            block(contrib, p * SEQS + row * 2 + 1 - c),
            block(from_core, p * 2 + row),
            rc_s.at[p * 2 + row],
            rc_r.at[p * 2 + row],
            at_core,
        )

    small = n // HALVES

    def piece(ref, index, h):
        return ref.at[pl.ds(pl.multiple_of(index * n + h * small, small), small)]

    def y_return(p, h):
        at = p * HALVES + h
        return put(
            piece(contrib, p * SEQS + (1 - y) * 2 + c, h),
            piece(from_y, p, h),
            ry_s.at[at],
            ry_r.at[at],
            at_y,
        )

    def z_return(p, slot, h, to):
        return put(
            piece(contrib, p * SEQS + place, h),
            piece(from_z, slot, h),
            rz_s.at[p * HALVES + h],
            rz_r.at[slot * HALVES + h],
            to,
        )

    shape = (pair, pair)
    earlier = lax.broadcasted_iota(jnp.int32, shape, 0)
    later = lax.broadcasted_iota(jnp.int32, shape, 1)
    before = (earlier < later) & (earlier // n == later // n)
    routed = gates_ref[...] > 0
    count = jnp.dot(
        routed.astype(jnp.bfloat16), before.astype(jnp.bfloat16), preferred_element_type=jnp.float32
    ).astype(jnp.int32)
    offset = lax.broadcasted_iota(jnp.int32, count.shape, 1) // n * cap
    ranks[...] = jnp.where(routed, count + offset, -1)

    def compute(p):
        parts = []
        for half in range(2):
            row = pl.ds(p * 2 + half, 1)
            hit = lax.broadcasted_iota(jnp.int32, (2 * cap, pair), 0) == ranks[row, :]
            gate = jnp.sum(jnp.where(hit, gates_ref[row, :], 0.0), axis=1, keepdims=True)
            choose = hit.astype(jnp.float32).astype(jnp.bfloat16)
            parts.append((choose, gate))
        tile = 512

        def pick(j, carry):
            cols = pl.ds(pl.multiple_of(j * tile, tile), tile)
            for half in range(2):
                source = pl.ds(pl.multiple_of((p * 2 + half) * pair, pair), pair)
                picked[pl.ds(half * 2 * cap, 2 * cap), cols] = jnp.dot(
                    parts[half][0], rows_all[source, cols], preferred_element_type=jnp.float32
                ).astype(jnp.bfloat16)
            return carry

        lax.fori_loop(0, width // tile, pick, 0)
        narrow = 256

        def gate_up(j, carry):
            first = pl.ds(pl.multiple_of(j * narrow, narrow), narrow)
            second = pl.ds(pl.multiple_of(hidden + j * narrow, narrow), narrow)
            v = jnp.dot(picked[...], w_up[:, first], preferred_element_type=jnp.float32)
            u = jnp.dot(picked[...], w_up[:, second], preferred_element_type=jnp.float32)
            act[:, first] = (v / (1.0 + jnp.exp(-v)) * u).astype(jnp.bfloat16)
            return carry

        lax.fori_loop(0, hidden // narrow, gate_up, 0)

        def down(j, carry):
            cols = pl.ds(pl.multiple_of(j * tile, tile), tile)
            result = jnp.dot(act[...], w_down[:, cols], preferred_element_type=jnp.float32)
            for half in range(2):
                choose, gate = parts[half]
                source = pl.ds(pl.multiple_of((p * 2 + half) * pair, pair), pair)
                part = result[half * 2 * cap : (half + 1) * 2 * cap] * gate
                contrib[source, cols] = lax.dot_general(
                    choose,
                    part.astype(jnp.bfloat16),
                    (((0,), (0,)), ((), ())),
                    preferred_element_type=jnp.float32,
                ).astype(jnp.bfloat16)
            return carry

        lax.fori_loop(0, width // tile, down, 0)

    chunk = 16

    def add_up(target, terms):
        def some(i, carry):
            here = pl.ds(pl.multiple_of(i * chunk, chunk), chunk)
            total = terms[0][here, :].astype(jnp.float32)
            for term in terms[1:]:
                total = total + term[here, :].astype(jnp.float32)
            target[here, :] = total.astype(target.dtype)
            return carry

        lax.fori_loop(0, small // chunk, some, 0)

    def core_sum(p):
        for row in range(2):
            core_return(p, row).wait_recv()
        for h in range(HALVES):
            other = piece(contrib, p * SEQS + (1 - y) * 2 + c, h)
            add_up(other, [other, piece(from_core, p * 2 + 1 - y, h)])
            y_return(p, h).start()

    def advance(k, carry):
        @pl.when(k < planes)
        def _():
            p = plane_at(k, z, planes)

            @pl.when(k > 0)
            def _():
                gather_copy(p * SEQS + place, y_s.at[p], at_y).wait_recv()

            start_all(forwards(p))

        j = k - lag

        @pl.when((j >= 0) & (j < planes))
        def _():
            p = plane_at(j, z, planes)
            second_forward(p).wait_recv()
            second_forward(p).start()
            pl.when(j == planes - 1)(lambda: core_sum(z))
            for row in range(2):
                gather_copy(p * SEQS + row * 2 + 1 - c, c_s.at[0], at_core).wait_recv()

            @pl.when(j == 0)
            def _():
                load_up.wait()
                load_down.wait()

            compute(p)
            for row in range(2):
                core_return(p, row).start()

        return carry

    lag = 1 + jnp.where(above & below, 1, 0)
    lax.fori_loop(0, planes + 2, advance, 0)
    def far_sum(i, carry):
        core_sum(plane_at(planes - 1 - i, z, planes))
        return carry

    lax.fori_loop(0, planes - 1, far_sum, 0)

    def chain(i, carry):
        p = plane_at(planes - 1 - i // HALVES, z, planes)
        h = i % HALVES
        y_return(p, h).wait_recv()
        own = piece(contrib, p * SEQS + place, h)
        terms = [own, piece(from_core, p * 2 + y, h), piece(from_y, p, h)]
        onward = ((p < z) & above) | ((p > z) & below)

        @pl.when(onward)
        def _():
            z_return(p, p, h, at_y).wait_recv()
            add_up(own, terms + [piece(from_z, p, h)])

        pl.when(jnp.logical_not(onward))(lambda: add_up(own, terms))

        @pl.when(p < z)
        def _():
            z_return(p, jnp.where(p == z - 1, planes, p), h, me - SEQS).start()

        @pl.when(p > z)
        def _():
            z_return(p, p, h, me + SEQS).start()

        return carry

    lax.fori_loop(0, (planes - 1) * HALVES, chain, 0)

    def last(h, carry):
        y_return(z, h).wait_recv()
        result = piece(out_ref, 0, h)
        terms = [
            piece(updated_ref, 0, h),
            piece(contrib, me, h),
            piece(from_core, z * 2 + y, h),
            piece(from_y, z, h),
        ]
        low, high = piece(from_z, z, h), piece(from_z, planes, h)
        pl.when(below)(lambda: z_return(z, z, h, at_y).wait_recv())
        pl.when(above)(lambda: z_return(z, planes, h, at_y).wait_recv())
        pl.when(below & above)(lambda: add_up(result, terms + [low, high]))
        pl.when(below & jnp.logical_not(above))(lambda: add_up(result, terms + [low]))
        pl.when(jnp.logical_not(below) & above)(lambda: add_up(result, terms + [high]))
        return carry

    lax.fori_loop(0, HALVES, last, 0)

    for by in range(1, planes):
        for copy in send_kv(by):
            copy.wait_send()
    tables_to_y().wait_send()
    tables_to_core().wait_send()

    def finish(p, carry):
        sent_all(column_forwards(p))
        pl.when(c == group)(column_seconds(p)[0].wait_send)
        column_seconds(p)[1].wait_send()
        sent_all(forwards(p))
        second_forward(p).wait_send()
        for row in range(2):
            core_return(p, row).wait_send()
        for h in range(HALVES):
            y_return(p, h).wait_send()

        @pl.when(p != z)
        def _():
            for h in range(HALVES):
                z_return(p, p, h, at_y).wait_send()

        return carry

    lax.fori_loop(0, planes, finish, 0)


def layer_call(
    order, residual, queries, keys, values, table, gain, out_weight, w_gate_up, w_down, cap
):
    n, width = residual.shape
    hidden = w_down.shape[1]
    devices = lax.axis_size("ctx")
    planes = devices // SEQS
    vmem = pl.BlockSpec(memory_space=pltpu.VMEM)
    anywhere = pl.BlockSpec(memory_space=pl.ANY)
    bf16 = jnp.bfloat16
    dma = pltpu.SemaphoreType.DMA
    return pl.pallas_call(
        functools.partial(layer_kernel, planes, cap),
        out_shape=[jax.ShapeDtypeStruct((n, width), bf16)] * 2,
        in_specs=[pl.BlockSpec(memory_space=pltpu.SMEM)] + [vmem] * 7 + [anywhere] * 2,
        out_specs=[vmem, vmem],
        scratch_shapes=[
            pltpu.VMEM((planes * n, 2 * keys.shape[1]), bf16),
            pltpu.VMEM((devices * devices, n), jnp.float32),
            pltpu.VMEM((2 * planes, 2 * n), jnp.float32),
            pltpu.VMEM((devices,) + out_weight.shape, bf16),
            pltpu.VMEM((n, width), jnp.float32),
            pltpu.VMEM((devices * n, width), bf16),
            pltpu.VMEM((devices * n, width), bf16),
            pltpu.VMEM((2 * planes * n, width), bf16),
            pltpu.VMEM((planes * n, width), bf16),
            pltpu.VMEM(((planes + 1) * n, width), bf16),
            pltpu.VMEM(w_gate_up.shape[1:], bf16),
            pltpu.VMEM(w_down.shape[1:], bf16),
            pltpu.VMEM((2 * planes, 2 * n), jnp.int32),
            pltpu.VMEM((SEQS * cap, width), bf16),
            pltpu.VMEM((SEQS * cap, hidden), bf16),
            dma((planes,)),
            dma((planes,)),
            dma((planes + 2,)),
            dma((planes + 2,)),
            dma((devices,)),
            dma((planes,)),
            dma((planes,)),
            dma((planes,)),
            dma((planes,)),
            dma((2 * planes,)),
            dma((2,)),
            dma((devices,)),
            dma((planes,)),
            dma((planes,)),
            dma((planes,)),
            dma((2 * planes,)),
            dma((2 * planes,)),
            dma((2 * planes,)),
            dma((HALVES * planes,)),
            dma((HALVES * planes,)),
            dma((HALVES * planes,)),
            dma((HALVES * (planes + 1),)),
        ],
        compiler_params=pltpu.CompilerParams(
            collective_id=0, has_side_effects=True, vmem_limit_bytes=VMEM_BYTES
        ),
        name="layer",
    )(order, residual, queries, keys, values, table, gain, out_weight, w_gate_up, w_down)


def gate_table(routes, route_weights, experts):
    gates = route_weights / jnp.sum(route_weights, axis=-1, keepdims=True)
    chosen = routes.T[None] == jnp.arange(experts, dtype=jnp.int32)[:, None, None]
    return jnp.sum(jnp.where(chosen, gates.T[None], 0.0), axis=1)


def fits(devices, rows, width, hidden):
    blocks = 4 * devices + 8
    return lax.axis_size("groups") == 2 and 2 * (blocks * rows * width + 3 * width * hidden) < VMEM_BYTES * 4 // 5


def local(
    residual,
    queries,
    keys,
    values,
    block_order,
    routes,
    route_weights,
    out_weight,
    norm_gain,
    w_gate_up,
    w_down,
):
    device_row_count = queries.shape[0]
    query_group_width = QUERY_HEADS // KEY_VALUE_HEADS
    devices = lax.axis_size("ctx")
    cycle_length = devices // SEQS
    own_index = lax.axis_index("ctx")
    experts = devices * w_gate_up.shape[0]
    capacity = 9 * device_row_count * TOPK // (8 * experts)
    if fits(devices, device_row_count, D, FF):
        return tuple(
            layer_call(
                block_order,
                residual,
                queries,
                keys,
                values,
                gate_table(routes, route_weights, experts),
                norm_gain.reshape(1, -1),
                out_weight,
                w_gate_up,
                w_down,
                capacity,
            )
        )
    full_weight = lax.all_gather(out_weight, "ctx", axis=1, tiled=True)
    query_position = block_order[own_index]
    query_head_rows = (
        queries.reshape(device_row_count, KEY_VALUE_HEADS, query_group_width, HEAD_SIZE)
        .transpose(1, 2, 0, 3)
        .reshape(KEY_VALUE_HEADS, query_group_width * device_row_count, HEAD_SIZE)
    )
    query_offset = jnp.arange(query_group_width * device_row_count) % device_row_count
    key_offset = jnp.arange(device_row_count)
    scale = HEAD_SIZE ** (-0.5)

    def update(carry, key_value_tuple, key_position):
        summed, running_max, totals = carry
        local_key_block = key_value_tuple[0].reshape(device_row_count, KEY_VALUE_HEADS, HEAD_SIZE)
        local_value_block = key_value_tuple[1].reshape(device_row_count, KEY_VALUE_HEADS, HEAD_SIZE)
        scores = (
            jnp.einsum(
                "hqd,khd->hqk", query_head_rows, local_key_block, preferred_element_type=jnp.float32
            )
            * scale
        )
        visible = (
            key_position * device_row_count + key_offset[None, :]
            <= query_position * device_row_count + query_offset[:, None]
        )
        scores = jnp.where(visible[None], scores, -jnp.inf)
        new_max = jnp.maximum(running_max, jnp.max(scores, axis=-1))
        factor = jnp.exp(running_max - new_max)
        weights = jnp.exp(scores - new_max[..., None])
        totals = totals * factor + jnp.sum(weights, axis=-1)
        summed = summed * factor[..., None] + jnp.einsum(
            "hqk,khd->hqd",
            weights.astype(jnp.bfloat16),
            local_value_block,
            preferred_element_type=jnp.float32,
        )
        return (summed, new_max, totals)

    initial = (
        jnp.zeros((KEY_VALUE_HEADS, query_group_width * device_row_count, HEAD_SIZE), jnp.float32),
        jnp.full((KEY_VALUE_HEADS, query_group_width * device_row_count), -jnp.inf, jnp.float32),
        jnp.zeros((KEY_VALUE_HEADS, query_group_width * device_row_count), jnp.float32),
    )
    local_pair = jnp.stack([keys, values])
    carry = update(initial, local_pair, query_position)

    def advance(step, state):
        current, moving = state
        moving = shifted(moving, "ctx", SEQS)
        anchor = jnp.mod(own_index - SEQS * step, devices)
        key_position = block_order[anchor]
        current = lax.cond(
            key_position <= query_position,
            lambda inner: update(inner, moving, key_position),
            lambda inner: inner,
            current,
        )
        return (current, moving)

    carry, passed = lax.fori_loop(1, cycle_length, advance, (carry, local_pair))
    summed, running_max, totals = carry
    context = (
        (summed / totals[..., None])
        .reshape(KEY_VALUE_HEADS, query_group_width, device_row_count, HEAD_SIZE)
        .transpose(2, 0, 1, 3)
        .reshape(device_row_count, QUERY_HEADS * HEAD_SIZE)
        .astype(jnp.bfloat16)
    )
    projected = jnp.dot(context, full_weight, preferred_element_type=jnp.float32)
    updated = residual.astype(jnp.float32) + projected
    normed = (
        updated * lax.rsqrt(jnp.mean(updated * updated, axis=-1, keepdims=True) + 1e-06) * norm_gain
    ).astype(jnp.bfloat16)
    experts = devices * w_gate_up.shape[0]
    capacity = 9 * device_row_count * TOPK // (8 * experts)
    expert_ids = routes.reshape(-1)
    one_hot = (expert_ids[:, None] == jnp.arange(experts, dtype=jnp.int32)[None, :]).astype(
        jnp.int32
    )
    ranks = jnp.sum(jnp.cumsum(one_hot, axis=0) * one_hot, axis=1) - 1
    target = expert_ids * capacity + ranks
    source_row = jnp.arange(device_row_count * TOPK) // TOPK
    outgoing = (
        jnp.zeros((experts * capacity, D), jnp.bfloat16)
        .at[target]
        .set(normed[source_row])
        .reshape(experts, capacity, D)
    )
    arrived = lax.all_to_all(outgoing, "ctx", split_axis=0, concat_axis=0, tiled=True)
    flat = arrived.reshape(-1, D)
    both = jnp.dot(flat, w_gate_up[0], preferred_element_type=jnp.float32)
    hidden = (jax.nn.silu(both[:, :FF]) * both[:, FF:]).astype(jnp.bfloat16)
    result = (
        jnp.dot(hidden, w_down[0], preferred_element_type=jnp.float32)
        .astype(jnp.bfloat16)
        .reshape(arrived.shape)
    )
    returned = lax.all_to_all(result, "ctx", split_axis=0, concat_axis=0, tiled=True)
    gathered = returned.reshape(-1, D)[target].reshape(device_row_count, TOPK, D)
    gates = route_weights / jnp.sum(route_weights, axis=-1, keepdims=True)
    mixed = updated
    for slot in range(TOPK):
        mixed = mixed + gates[:, slot : slot + 1] * gathered[:, slot].astype(jnp.float32)
    return (context, mixed.astype(jnp.bfloat16))


def solution(mesh):
    placed = (
        P(("groups", "ctx"), None),
        P(("groups", "ctx"), None),
        P(("groups", "ctx"), None),
        P(("groups", "ctx"), None),
        P("groups"),
        P(("groups", "ctx"), None),
        P(("groups", "ctx"), None),
        P(None, "ctx"),
        P(),
        P("ctx", None, None),
        P("ctx", None, None),
    )
    return jax.shard_map(
        local,
        mesh=mesh,
        in_specs=placed,
        out_specs=(P(("groups", "ctx"), None), P(("groups", "ctx"), None)),
        check_vma=False,
    )
```

```python
import functools

import jax
import jax.numpy as jnp
from jax import lax
from jax.experimental import pallas as pl
from jax.experimental.pallas import tpu as pltpu
from jax.sharding import PartitionSpec as P

D = 2048
HEAD_SIZE = 128
FF = 768
QUERY_HEADS = 16
KEY_VALUE_HEADS = 2
TOPK = 8
SEQS = 4


def shifted(array, axis, by):
    devices = lax.axis_size(axis)
    return lax.ppermute(array, axis, [(i, (i + by) % devices) for i in range(devices)])


VMEM_BYTES = 60 * 2**20
HALVES = 4


def put(src, dst, send_sem, recv_sem, to, axis="ctx"):
    return pltpu.make_async_remote_copy(
        src_ref=src,
        dst_ref=dst,
        send_sem=send_sem,
        recv_sem=recv_sem,
        device_id={axis: to},
        device_id_type=pl.DeviceIdType.MESH,
    )


def plane_at(step, z, planes):
    short = jnp.minimum(z, planes - 1 - z)
    sign = jnp.where(2 * z < planes - 1, 1, -1)
    near = (step + 1) // 2 * (2 * (step % 2) - 1)
    return z + sign * jnp.where(step <= 2 * short, near, step - short)


def layer_kernel(
    planes,
    cap,
    order_ref,
    residual_ref,
    queries_ref,
    keys_ref,
    values_ref,
    routes_ref,
    shares_ref,
    gain_ref,
    weight_ref,
    up_hbm,
    down_hbm,
    context_ref,
    out_ref,
    kv,
    tables,
    gates_ref,
    columns,
    updated_ref,
    rows_all,
    contrib,
    from_core,
    from_y,
    from_z,
    w_up,
    w_down,
    ranks,
    picked,
    act,
    kv_s,
    kv_r,
    t_s,
    t_r,
    o_recv,
    o_up_s,
    o_dn_s,
    o_y_s,
    o_x_s,
    o_c_s,
    o_far_s,
    w_sem,
    recv,
    up_s,
    dn_s,
    y_s,
    c_s,
    rc_s,
    rc_r,
    ry_s,
    ry_r,
    rz_s,
    rz_r,
):
    n, width = residual_ref.shape
    hidden = w_down.shape[0]
    pair = 2 * n
    me = lax.axis_index("ctx")
    z, place = me // SEQS, me % SEQS
    y, c = place // 2, place % 2
    at_y = z * SEQS + (1 - y) * 2 + c
    at_core = z * SEQS + y * 2 + (1 - c)
    above, below = z < planes - 1, z > 0

    def block(ref, index):
        return ref.at[pl.ds(pl.multiple_of(index * n, n), n)]

    load_up = pltpu.make_async_copy(up_hbm.at[0], w_up, w_sem.at[0])
    load_down = pltpu.make_async_copy(down_hbm.at[0], w_down, w_sem.at[1])
    load_up.start()
    load_down.start()

    barrier = pltpu.get_barrier_semaphore()

    def greet(to, axis="ctx"):
        pl.semaphore_signal(
            barrier, inc=1, device_id={axis: to}, device_id_type=pl.DeviceIdType.MESH
        )

    group = lax.axis_index("groups")
    at_x = 1 - group
    experts = planes * SEQS
    greet(at_x, "groups")
    greet(at_y)
    greet(at_core)
    for by in range(1, planes):
        greet(lax.rem(z + by, planes) * SEQS + place)
    kv_width = keys_ref.shape[1]
    own_kv = block(kv, z)
    own_kv[:, :kv_width] = keys_ref[...]
    own_kv[:, kv_width:] = values_ref[...]
    column = c * 2 + y

    def table(col, plane, count):
        start = pl.multiple_of((col * planes + plane) * experts, experts)
        return tables.at[pl.ds(start, count * experts)]

    shares = shares_ref[...]
    gates = shares / jnp.sum(shares, axis=1, keepdims=True)
    expert_lane = lax.broadcasted_iota(jnp.int32, (n, HEAD_SIZE), 1)
    spread = jnp.zeros((n, HEAD_SIZE), jnp.float32)
    for slot in range(shares_ref.shape[1]):
        spread = spread + jnp.where(
            routes_ref[:, slot : slot + 1] == expert_lane, gates[:, slot : slot + 1], 0.0
        )
    table(column, z, 1)[...] = spread.T[:experts]
    columns[me] = weight_ref[...]
    pl.semaphore_wait(barrier, planes + 2)

    def kv_copy(plane, by):
        return put(block(kv, plane), block(kv, plane), kv_s.at[by], kv_r.at[plane], at_y)

    def send_kv(by):
        to = lax.rem(z + by, planes) * SEQS + place
        return (
            put(own_kv, own_kv, kv_s.at[by], kv_r.at[z], to),
            put(table(column, z, 1), table(column, z, 1), t_s.at[by], t_r.at[z], to),
        )

    def tables_to_y():
        part = table(column, 0, planes)
        return put(part, part, t_s.at[planes], t_r.at[planes], at_y)

    def tables_to_core():
        part = table(c * 2, 0, 2 * planes)
        return put(part, part, t_s.at[planes + 1], t_r.at[planes + 1], at_core)

    for by in range(1, planes):
        for copy in send_kv(by):
            copy.start()

    def column_copy(index, sem, to, axis="ctx"):
        return put(columns.at[index], columns.at[index], sem, o_recv.at[index], to, axis)

    def column_forwards(p):
        index = p * SEQS + place
        keep = c == group
        up = above & (p <= z) & (keep | (p > 0) | (z + 2 < planes))
        down = below & (p >= z) & (keep | (p < planes - 1) | (z > 1))
        ends = ((z == 0) & (p == planes - 1)) | ((z == planes - 1) & (p == 0))
        return (
            (up, column_copy(index, o_up_s.at[p], me + SEQS)),
            (down, column_copy(index, o_dn_s.at[p], me - SEQS)),
            (keep & ends, column_copy(index, o_far_s, at_x, "groups")),
            (c == group, column_copy(index, o_y_s.at[p], at_y)),
            (None, column_copy(index, o_c_s.at[p * 2 + y], at_core)),
        )

    def column_seconds(p):
        index = p * SEQS + (1 - y) * 2 + c
        return (
            column_copy(index, o_x_s.at[p], at_x, "groups"),
            column_copy(index, o_c_s.at[p * 2 + 1 - y], at_core),
        )

    def start_all(copies):
        for condition, copy in copies:
            if condition is None:
                copy.start()
            else:
                pl.when(condition)(copy.start)

    def sent_all(copies):
        for condition, copy in copies:
            if condition is None:
                copy.wait_send()
            else:
                pl.when(condition)(copy.wait_send)

    start_all(column_forwards(z))
    for by in range(1, planes):
        plane = lax.rem(z + by, planes)
        kv_copy(plane, by).wait_recv()
        put(
            table(column, plane, 1), table(column, plane, 1), t_s.at[by], t_r.at[plane], at_y
        ).wait_recv()
    tables_to_y().start()

    total_keys = planes * n
    lane = lax.broadcasted_iota(jnp.int32, (n, total_keys), 1)
    key_plane = lane // n
    key_position = lane % n
    for plane in range(planes):
        key_position = key_position + jnp.where(
            key_plane == plane, order_ref[plane * SEQS + place] * n, 0
        )
    query_position = order_ref[me] * n + lax.broadcasted_iota(jnp.int32, (n, total_keys), 0)
    visible = key_position <= query_position
    heads = width // HEAD_SIZE
    kv_heads = kv_width // HEAD_SIZE

    def attend(head, carry):
        cols = pl.ds(pl.multiple_of(head * HEAD_SIZE, HEAD_SIZE), HEAD_SIZE)
        kv_head = head // (heads // kv_heads)
        key_cols = pl.ds(pl.multiple_of(kv_head * HEAD_SIZE, HEAD_SIZE), HEAD_SIZE)
        value_cols = pl.ds(pl.multiple_of(kv_width + kv_head * HEAD_SIZE, HEAD_SIZE), HEAD_SIZE)
        scores = lax.dot_general(
            queries_ref[:, cols],
            kv[:, key_cols],
            (((1,), (1,)), ((), ())),
            preferred_element_type=jnp.float32,
        ) * (HEAD_SIZE**-0.5)
        scores = jnp.where(visible, scores, -jnp.inf)
        weights = jnp.exp(scores - jnp.max(scores, axis=1, keepdims=True))
        total = jnp.sum(weights, axis=1, keepdims=True)
        summed = jnp.dot(
            weights.astype(jnp.bfloat16), kv[:, value_cols], preferred_element_type=jnp.float32
        )
        context_ref[:, cols] = (summed / total).astype(jnp.bfloat16)
        return carry

    lax.fori_loop(0, heads, attend, 0, unroll=4)
    tables_to_y().wait_recv()
    tables_to_core().start()

    def weight_step(k, carry):
        @pl.when(k < planes)
        def _():
            p = plane_at(k, z, planes)
            column_copy(p * SEQS + place, o_y_s.at[p], at_y).wait_recv()
            start_all(column_forwards(p))

        @pl.when((k <= planes) & (c == group))
        def _():
            p = plane_at(k - 1, z, planes)
            column_copy(p * SEQS + (1 - y) * 2 + c, o_y_s.at[p], at_y).wait_recv()
            for copy in column_seconds(p):
                copy.start()

        @pl.when(k > 1)
        def _():
            p = plane_at(k - 2, z, planes)

            @pl.when(c != group)
            def _():
                column_copy(p * SEQS + (1 - y) * 2 + c, o_y_s.at[p], at_y).wait_recv()
                column_seconds(p)[1].start()

            for row in range(2):
                column_copy(p * SEQS + row * 2 + 1 - c, o_y_s.at[p], at_core).wait_recv()
            for spot in range(SEQS):
                index = p * SEQS + spot
                each = columns.shape[2]
                cols = pl.ds(pl.multiple_of(index * each, each), each)
                updated_ref[:, cols] = residual_ref[:, cols].astype(jnp.float32) + jnp.dot(
                    context_ref[...], columns[index], preferred_element_type=jnp.float32
                )

        return carry

    lax.fori_loop(1, planes + 2, weight_step, 0)
    tables_to_core().wait_recv()

    def norm(i, carry):
        rows = pl.ds(pl.multiple_of(i * 16, 16), 16)
        rows_there = pl.ds(pl.multiple_of(me * n + i * 16, 16), 16)
        updated = updated_ref[rows, :]
        mean = jnp.mean(updated * updated, axis=1, keepdims=True)
        rows_all[rows_there, :] = (updated * lax.rsqrt(mean + 1e-06) * gain_ref[...]).astype(
            jnp.bfloat16
        )
        return carry

    lax.fori_loop(0, n // 16, norm, 0)
    for p in range(planes):
        for row in range(2):
            for core in range(2):
                at = ((core * 2 + row) * planes + p) * experts + me
                gates_ref[pl.ds(p * 2 + row, 1), pl.ds(core * n, n)] = tables[pl.ds(at, 1), :]

    def gather_copy(index, sem, to):
        return put(block(rows_all, index), block(rows_all, index), sem, recv.at[index], to)

    def forwards(p):
        index = p * SEQS + place
        return (
            (above & (p <= z), gather_copy(index, up_s.at[p], me + SEQS)),
            (below & (p >= z), gather_copy(index, dn_s.at[p], me - SEQS)),
            (None, gather_copy(index, y_s.at[p], at_y)),
            (None, gather_copy(index, c_s.at[p * 2 + y], at_core)),
        )

    def second_forward(p):
        return gather_copy(p * SEQS + (1 - y) * 2 + c, c_s.at[p * 2 + 1 - y], at_core)

    def core_return(p, row):
        return put(
            block(contrib, p * SEQS + row * 2 + 1 - c),
            block(from_core, p * 2 + row),
            rc_s.at[p * 2 + row],
            rc_r.at[p * 2 + row],
            at_core,
        )

    small = n // HALVES

    def piece(ref, index, h):
        return ref.at[pl.ds(pl.multiple_of(index * n + h * small, small), small)]

    def y_return(p, h):
        at = p * HALVES + h
        return put(
            piece(contrib, p * SEQS + (1 - y) * 2 + c, h),
            piece(from_y, p, h),
            ry_s.at[at],
            ry_r.at[at],
            at_y,
        )

    def z_return(p, slot, h, to):
        return put(
            piece(contrib, p * SEQS + place, h),
            piece(from_z, slot, h),
            rz_s.at[p * HALVES + h],
            rz_r.at[slot * HALVES + h],
            to,
        )

    shape = (pair, pair)
    earlier = lax.broadcasted_iota(jnp.int32, shape, 0)
    later = lax.broadcasted_iota(jnp.int32, shape, 1)
    before = (earlier < later) & (earlier // n == later // n)
    routed = gates_ref[...] > 0
    count = jnp.dot(
        routed.astype(jnp.bfloat16), before.astype(jnp.bfloat16), preferred_element_type=jnp.float32
    ).astype(jnp.int32)
    offset = lax.broadcasted_iota(jnp.int32, count.shape, 1) // n * cap
    ranks[...] = jnp.where(routed, count + offset, -1)

    def compute(p):
        parts = []
        for half in range(2):
            row = pl.ds(p * 2 + half, 1)
            hit = lax.broadcasted_iota(jnp.int32, (2 * cap, pair), 0) == ranks[row, :]
            gate = jnp.sum(jnp.where(hit, gates_ref[row, :], 0.0), axis=1, keepdims=True)
            choose = hit.astype(jnp.float32).astype(jnp.bfloat16)
            parts.append((choose, gate))
        tile = 512

        def pick(j, carry):
            cols = pl.ds(pl.multiple_of(j * tile, tile), tile)
            for half in range(2):
                source = pl.ds(pl.multiple_of((p * 2 + half) * pair, pair), pair)
                picked[pl.ds(half * 2 * cap, 2 * cap), cols] = jnp.dot(
                    parts[half][0], rows_all[source, cols], preferred_element_type=jnp.float32
                ).astype(jnp.bfloat16)
            return carry

        lax.fori_loop(0, width // tile, pick, 0)
        narrow = 256

        def gate_up(j, carry):
            first = pl.ds(pl.multiple_of(j * narrow, narrow), narrow)
            second = pl.ds(pl.multiple_of(hidden + j * narrow, narrow), narrow)
            v = jnp.dot(picked[...], w_up[:, first], preferred_element_type=jnp.float32)
            u = jnp.dot(picked[...], w_up[:, second], preferred_element_type=jnp.float32)
            act[:, first] = (v / (1.0 + jnp.exp(-v)) * u).astype(jnp.bfloat16)
            return carry

        lax.fori_loop(0, hidden // narrow, gate_up, 0)

        def down(j, carry):
            cols = pl.ds(pl.multiple_of(j * tile, tile), tile)
            result = jnp.dot(act[...], w_down[:, cols], preferred_element_type=jnp.float32)
            for half in range(2):
                choose, gate = parts[half]
                source = pl.ds(pl.multiple_of((p * 2 + half) * pair, pair), pair)
                part = result[half * 2 * cap : (half + 1) * 2 * cap] * gate
                contrib[source, cols] = lax.dot_general(
                    choose,
                    part.astype(jnp.bfloat16),
                    (((0,), (0,)), ((), ())),
                    preferred_element_type=jnp.float32,
                ).astype(jnp.bfloat16)
            return carry

        lax.fori_loop(0, width // tile, down, 0)

    chunk = 16

    def add_up(target, terms):
        def some(i, carry):
            here = pl.ds(pl.multiple_of(i * chunk, chunk), chunk)
            total = terms[0][here, :].astype(jnp.float32)
            for term in terms[1:]:
                total = total + term[here, :].astype(jnp.float32)
            target[here, :] = total.astype(target.dtype)
            return carry

        lax.fori_loop(0, small // chunk, some, 0)

    def core_sum(p):
        for row in range(2):
            core_return(p, row).wait_recv()
        for h in range(HALVES):
            other = piece(contrib, p * SEQS + (1 - y) * 2 + c, h)
            add_up(other, [other, piece(from_core, p * 2 + 1 - y, h)])
            y_return(p, h).start()

    def advance(k, carry):
        @pl.when(k < planes)
        def _():
            p = plane_at(k, z, planes)

            @pl.when(k > 0)
            def _():
                gather_copy(p * SEQS + place, y_s.at[p], at_y).wait_recv()

            start_all(forwards(p))

        j = k - lag

        @pl.when((j >= 0) & (j < planes))
        def _():
            p = plane_at(j, z, planes)
            second_forward(p).wait_recv()
            second_forward(p).start()
            pl.when(j == planes - 1)(lambda: core_sum(z))
            for row in range(2):
                gather_copy(p * SEQS + row * 2 + 1 - c, c_s.at[0], at_core).wait_recv()

            @pl.when(j == 0)
            def _():
                load_up.wait()
                load_down.wait()

            compute(p)
            for row in range(2):
                core_return(p, row).start()

        return carry

    lag = 1 + jnp.where(above & below, 1, 0)
    lax.fori_loop(0, planes + 2, advance, 0)
    def far_sum(i, carry):
        core_sum(plane_at(planes - 1 - i, z, planes))
        return carry

    lax.fori_loop(0, planes - 1, far_sum, 0)

    def chain(i, carry):
        p = plane_at(planes - 1 - i // HALVES, z, planes)
        h = i % HALVES
        y_return(p, h).wait_recv()
        own = piece(contrib, p * SEQS + place, h)
        terms = [own, piece(from_core, p * 2 + y, h), piece(from_y, p, h)]
        onward = ((p < z) & above) | ((p > z) & below)

        @pl.when(onward)
        def _():
            z_return(p, p, h, at_y).wait_recv()
            add_up(own, terms + [piece(from_z, p, h)])

        pl.when(jnp.logical_not(onward))(lambda: add_up(own, terms))

        @pl.when(p < z)
        def _():
            z_return(p, jnp.where(p == z - 1, planes, p), h, me - SEQS).start()

        @pl.when(p > z)
        def _():
            z_return(p, p, h, me + SEQS).start()

        return carry

    lax.fori_loop(0, (planes - 1) * HALVES, chain, 0)

    def last(h, carry):
        y_return(z, h).wait_recv()
        result = piece(out_ref, 0, h)
        terms = [
            piece(updated_ref, 0, h),
            piece(contrib, me, h),
            piece(from_core, z * 2 + y, h),
            piece(from_y, z, h),
        ]
        low, high = piece(from_z, z, h), piece(from_z, planes, h)
        pl.when(below)(lambda: z_return(z, z, h, at_y).wait_recv())
        pl.when(above)(lambda: z_return(z, planes, h, at_y).wait_recv())
        pl.when(below & above)(lambda: add_up(result, terms + [low, high]))
        pl.when(below & jnp.logical_not(above))(lambda: add_up(result, terms + [low]))
        pl.when(jnp.logical_not(below) & above)(lambda: add_up(result, terms + [high]))
        return carry

    lax.fori_loop(0, HALVES, last, 0)

    for by in range(1, planes):
        for copy in send_kv(by):
            copy.wait_send()
    tables_to_y().wait_send()
    tables_to_core().wait_send()

    def finish(p, carry):
        sent_all(column_forwards(p))
        pl.when(c == group)(column_seconds(p)[0].wait_send)
        column_seconds(p)[1].wait_send()
        sent_all(forwards(p))
        second_forward(p).wait_send()
        for row in range(2):
            core_return(p, row).wait_send()
        for h in range(HALVES):
            y_return(p, h).wait_send()

        @pl.when(p != z)
        def _():
            for h in range(HALVES):
                z_return(p, p, h, at_y).wait_send()

        return carry

    lax.fori_loop(0, planes, finish, 0)


def layer_call(
    order,
    residual,
    queries,
    keys,
    values,
    routes,
    shares,
    gain,
    out_weight,
    w_gate_up,
    w_down,
    cap,
):
    n, width = residual.shape
    hidden = w_down.shape[1]
    devices = lax.axis_size("ctx")
    planes = devices // SEQS
    vmem = pl.BlockSpec(memory_space=pltpu.VMEM)
    anywhere = pl.BlockSpec(memory_space=pl.ANY)
    bf16 = jnp.bfloat16
    dma = pltpu.SemaphoreType.DMA
    return pl.pallas_call(
        functools.partial(layer_kernel, planes, cap),
        out_shape=[jax.ShapeDtypeStruct((n, width), bf16)] * 2,
        in_specs=[pl.BlockSpec(memory_space=pltpu.SMEM)] + [vmem] * 8 + [anywhere] * 2,
        out_specs=[vmem, vmem],
        scratch_shapes=[
            pltpu.VMEM((planes * n, 2 * keys.shape[1]), bf16),
            pltpu.VMEM((devices * devices, n), jnp.float32),
            pltpu.VMEM((2 * planes, 2 * n), jnp.float32),
            pltpu.VMEM((devices,) + out_weight.shape, bf16),
            pltpu.VMEM((n, width), jnp.float32),
            pltpu.VMEM((devices * n, width), bf16),
            pltpu.VMEM((devices * n, width), bf16),
            pltpu.VMEM((2 * planes * n, width), bf16),
            pltpu.VMEM((planes * n, width), bf16),
            pltpu.VMEM(((planes + 1) * n, width), bf16),
            pltpu.VMEM(w_gate_up.shape[1:], bf16),
            pltpu.VMEM(w_down.shape[1:], bf16),
            pltpu.VMEM((2 * planes, 2 * n), jnp.int32),
            pltpu.VMEM((SEQS * cap, width), bf16),
            pltpu.VMEM((SEQS * cap, hidden), bf16),
            dma((planes,)),
            dma((planes,)),
            dma((planes + 2,)),
            dma((planes + 2,)),
            dma((devices,)),
            dma((planes,)),
            dma((planes,)),
            dma((planes,)),
            dma((planes,)),
            dma((2 * planes,)),
            dma,
            dma((2,)),
            dma((devices,)),
            dma((planes,)),
            dma((planes,)),
            dma((planes,)),
            dma((2 * planes,)),
            dma((2 * planes,)),
            dma((2 * planes,)),
            dma((HALVES * planes,)),
            dma((HALVES * planes,)),
            dma((HALVES * planes,)),
            dma((HALVES * (planes + 1),)),
        ],
        compiler_params=pltpu.CompilerParams(
            collective_id=0, has_side_effects=True, vmem_limit_bytes=VMEM_BYTES
        ),
        name="layer",
    )(order, residual, queries, keys, values, routes, shares, gain, out_weight, w_gate_up, w_down)


def fits(devices, rows, width, hidden):
    blocks = 4 * devices + 8
    return lax.axis_size("groups") == 2 and 2 * (blocks * rows * width + 3 * width * hidden) < VMEM_BYTES * 4 // 5


def local(
    residual,
    queries,
    keys,
    values,
    block_order,
    routes,
    route_weights,
    out_weight,
    norm_gain,
    w_gate_up,
    w_down,
):
    device_row_count = queries.shape[0]
    query_group_width = QUERY_HEADS // KEY_VALUE_HEADS
    devices = lax.axis_size("ctx")
    cycle_length = devices // SEQS
    own_index = lax.axis_index("ctx")
    experts = devices * w_gate_up.shape[0]
    capacity = 9 * device_row_count * TOPK // (8 * experts)
    if fits(devices, device_row_count, D, FF):
        return tuple(
            layer_call(
                block_order,
                residual,
                queries,
                keys,
                values,
                routes,
                route_weights,
                norm_gain.reshape(1, -1),
                out_weight,
                w_gate_up,
                w_down,
                capacity,
            )
        )
    full_weight = lax.all_gather(out_weight, "ctx", axis=1, tiled=True)
    query_position = block_order[own_index]
    query_head_rows = (
        queries.reshape(device_row_count, KEY_VALUE_HEADS, query_group_width, HEAD_SIZE)
        .transpose(1, 2, 0, 3)
        .reshape(KEY_VALUE_HEADS, query_group_width * device_row_count, HEAD_SIZE)
    )
    query_offset = jnp.arange(query_group_width * device_row_count) % device_row_count
    key_offset = jnp.arange(device_row_count)
    scale = HEAD_SIZE ** (-0.5)

    def update(carry, key_value_tuple, key_position):
        summed, running_max, totals = carry
        local_key_block = key_value_tuple[0].reshape(device_row_count, KEY_VALUE_HEADS, HEAD_SIZE)
        local_value_block = key_value_tuple[1].reshape(device_row_count, KEY_VALUE_HEADS, HEAD_SIZE)
        scores = (
            jnp.einsum(
                "hqd,khd->hqk", query_head_rows, local_key_block, preferred_element_type=jnp.float32
            )
            * scale
        )
        visible = (
            key_position * device_row_count + key_offset[None, :]
            <= query_position * device_row_count + query_offset[:, None]
        )
        scores = jnp.where(visible[None], scores, -jnp.inf)
        new_max = jnp.maximum(running_max, jnp.max(scores, axis=-1))
        factor = jnp.exp(running_max - new_max)
        weights = jnp.exp(scores - new_max[..., None])
        totals = totals * factor + jnp.sum(weights, axis=-1)
        summed = summed * factor[..., None] + jnp.einsum(
            "hqk,khd->hqd",
            weights.astype(jnp.bfloat16),
            local_value_block,
            preferred_element_type=jnp.float32,
        )
        return (summed, new_max, totals)

    initial = (
        jnp.zeros((KEY_VALUE_HEADS, query_group_width * device_row_count, HEAD_SIZE), jnp.float32),
        jnp.full((KEY_VALUE_HEADS, query_group_width * device_row_count), -jnp.inf, jnp.float32),
        jnp.zeros((KEY_VALUE_HEADS, query_group_width * device_row_count), jnp.float32),
    )
    local_pair = jnp.stack([keys, values])
    carry = update(initial, local_pair, query_position)

    def advance(step, state):
        current, moving = state
        moving = shifted(moving, "ctx", SEQS)
        anchor = jnp.mod(own_index - SEQS * step, devices)
        key_position = block_order[anchor]
        current = lax.cond(
            key_position <= query_position,
            lambda inner: update(inner, moving, key_position),
            lambda inner: inner,
            current,
        )
        return (current, moving)

    carry, passed = lax.fori_loop(1, cycle_length, advance, (carry, local_pair))
    summed, running_max, totals = carry
    context = (
        (summed / totals[..., None])
        .reshape(KEY_VALUE_HEADS, query_group_width, device_row_count, HEAD_SIZE)
        .transpose(2, 0, 1, 3)
        .reshape(device_row_count, QUERY_HEADS * HEAD_SIZE)
        .astype(jnp.bfloat16)
    )
    projected = jnp.dot(context, full_weight, preferred_element_type=jnp.float32)
    updated = residual.astype(jnp.float32) + projected
    normed = (
        updated * lax.rsqrt(jnp.mean(updated * updated, axis=-1, keepdims=True) + 1e-06) * norm_gain
    ).astype(jnp.bfloat16)
    experts = devices * w_gate_up.shape[0]
    capacity = 9 * device_row_count * TOPK // (8 * experts)
    expert_ids = routes.reshape(-1)
    one_hot = (expert_ids[:, None] == jnp.arange(experts, dtype=jnp.int32)[None, :]).astype(
        jnp.int32
    )
    ranks = jnp.sum(jnp.cumsum(one_hot, axis=0) * one_hot, axis=1) - 1
    target = expert_ids * capacity + ranks
    source_row = jnp.arange(device_row_count * TOPK) // TOPK
    outgoing = (
        jnp.zeros((experts * capacity, D), jnp.bfloat16)
        .at[target]
        .set(normed[source_row])
        .reshape(experts, capacity, D)
    )
    arrived = lax.all_to_all(outgoing, "ctx", split_axis=0, concat_axis=0, tiled=True)
    flat = arrived.reshape(-1, D)
    both = jnp.dot(flat, w_gate_up[0], preferred_element_type=jnp.float32)
    hidden = (jax.nn.silu(both[:, :FF]) * both[:, FF:]).astype(jnp.bfloat16)
    result = (
        jnp.dot(hidden, w_down[0], preferred_element_type=jnp.float32)
        .astype(jnp.bfloat16)
        .reshape(arrived.shape)
    )
    returned = lax.all_to_all(result, "ctx", split_axis=0, concat_axis=0, tiled=True)
    gathered = returned.reshape(-1, D)[target].reshape(device_row_count, TOPK, D)
    gates = route_weights / jnp.sum(route_weights, axis=-1, keepdims=True)
    mixed = updated
    for slot in range(TOPK):
        mixed = mixed + gates[:, slot : slot + 1] * gathered[:, slot].astype(jnp.float32)
    return (context, mixed.astype(jnp.bfloat16))


def solution(mesh):
    placed = (
        P(("groups", "ctx"), None),
        P(("groups", "ctx"), None),
        P(("groups", "ctx"), None),
        P(("groups", "ctx"), None),
        P("groups"),
        P(("groups", "ctx"), None),
        P(("groups", "ctx"), None),
        P(None, "ctx"),
        P(),
        P("ctx", None, None),
        P("ctx", None, None),
    )
    return jax.shard_map(
        local,
        mesh=mesh,
        in_specs=placed,
        out_specs=(P(("groups", "ctx"), None), P(("groups", "ctx"), None)),
        check_vma=False,
    )
```

```python
import functools

import jax
import jax.numpy as jnp
from jax import lax
from jax.experimental import pallas as pl
from jax.experimental.pallas import tpu as pltpu
from jax.sharding import PartitionSpec as P

D = 2048
HEAD_SIZE = 128
FF = 768
QUERY_HEADS = 16
KEY_VALUE_HEADS = 2
TOPK = 8
SEQS = 4


def shifted(array, axis, by):
    devices = lax.axis_size(axis)
    return lax.ppermute(array, axis, [(i, (i + by) % devices) for i in range(devices)])


VMEM_BYTES = 60 * 2**20
HALVES = 4


def put(src, dst, send_sem, recv_sem, to, axis="ctx"):
    return pltpu.make_async_remote_copy(
        src_ref=src,
        dst_ref=dst,
        send_sem=send_sem,
        recv_sem=recv_sem,
        device_id={axis: to},
        device_id_type=pl.DeviceIdType.MESH,
    )


def plane_at(step, z, planes):
    short = jnp.minimum(z, planes - 1 - z)
    sign = jnp.where(2 * z < planes - 1, 1, -1)
    near = (step + 1) // 2 * (2 * (step % 2) - 1)
    return z + sign * jnp.where(step <= 2 * short, near, step - short)


def layer_kernel(
    planes,
    cap,
    order_ref,
    residual_ref,
    queries_ref,
    keys_ref,
    values_ref,
    choices_ref,
    gain_ref,
    weight_ref,
    up_hbm,
    down_hbm,
    context_ref,
    out_ref,
    kv,
    tables,
    gates_ref,
    columns,
    updated_ref,
    rows_all,
    contrib,
    from_core,
    from_y,
    from_z,
    w_up,
    w_down,
    ranks,
    picked,
    act,
    kv_s,
    kv_r,
    t_s,
    t_r,
    o_recv,
    o_up_s,
    o_dn_s,
    o_y_s,
    o_x_s,
    o_c_s,
    o_far_s,
    w_sem,
    recv,
    up_s,
    dn_s,
    y_s,
    c_s,
    rc_s,
    rc_r,
    ry_s,
    ry_r,
    rz_s,
    rz_r,
):
    n, width = residual_ref.shape
    hidden = w_down.shape[0]
    pair = 2 * n
    me = lax.axis_index("ctx")
    z, place = me // SEQS, me % SEQS
    y, c = place // 2, place % 2
    at_y = z * SEQS + (1 - y) * 2 + c
    at_core = z * SEQS + y * 2 + (1 - c)
    above, below = z < planes - 1, z > 0

    def block(ref, index):
        return ref.at[pl.ds(pl.multiple_of(index * n, n), n)]

    load_up = pltpu.make_async_copy(up_hbm.at[0], w_up, w_sem.at[0])
    load_down = pltpu.make_async_copy(down_hbm.at[0], w_down, w_sem.at[1])
    load_up.start()
    load_down.start()

    barrier = pltpu.get_barrier_semaphore()

    def greet(to, axis="ctx"):
        pl.semaphore_signal(
            barrier, inc=1, device_id={axis: to}, device_id_type=pl.DeviceIdType.MESH
        )

    group = lax.axis_index("groups")
    at_x = 1 - group
    experts = planes * SEQS
    greet(at_x, "groups")
    greet(at_y)
    greet(at_core)
    for by in range(1, planes):
        greet(lax.rem(z + by, planes) * SEQS + place)
    kv_width = keys_ref.shape[1]
    own_kv = block(kv, z)
    own_kv[:, :kv_width] = keys_ref[...]
    own_kv[:, kv_width:] = values_ref[...]
    column = c * 2 + y

    def table(col, plane, count):
        start = pl.multiple_of((col * planes + plane) * experts, experts)
        return tables.at[pl.ds(start, count * experts)]

    slots = choices_ref.shape[1] // 2
    routes, shares = choices_ref[:, :slots], choices_ref[:, slots:]
    gates = shares / jnp.sum(shares, axis=1, keepdims=True)
    expert_lane = lax.broadcasted_iota(jnp.int32, (n, HEAD_SIZE), 1).astype(jnp.float32)
    spread = jnp.zeros((n, HEAD_SIZE), jnp.float32)
    for slot in range(slots):
        spread = spread + jnp.where(
            routes[:, slot : slot + 1] == expert_lane, gates[:, slot : slot + 1], 0.0
        )
    table(column, z, 1)[...] = spread.T[:experts]
    columns[me] = weight_ref[...]
    pl.semaphore_wait(barrier, planes + 2)

    def kv_copy(plane, by):
        return put(block(kv, plane), block(kv, plane), kv_s.at[by], kv_r.at[plane], at_y)

    def send_kv(by):
        to = lax.rem(z + by, planes) * SEQS + place
        return (
            put(own_kv, own_kv, kv_s.at[by], kv_r.at[z], to),
            put(table(column, z, 1), table(column, z, 1), t_s.at[by], t_r.at[z], to),
        )

    def tables_to_y():
        part = table(column, 0, planes)
        return put(part, part, t_s.at[planes], t_r.at[planes], at_y)

    def tables_to_core():
        part = table(c * 2, 0, 2 * planes)
        return put(part, part, t_s.at[planes + 1], t_r.at[planes + 1], at_core)

    for by in range(1, planes):
        for copy in send_kv(by):
            copy.start()

    def column_copy(index, sem, to, axis="ctx"):
        return put(columns.at[index], columns.at[index], sem, o_recv.at[index], to, axis)

    def column_forwards(p):
        index = p * SEQS + place
        keep = c == group
        up = above & (p <= z) & (keep | (p > 0) | (z + 2 < planes))
        down = below & (p >= z) & (keep | (p < planes - 1) | (z > 1))
        ends = ((z == 0) & (p == planes - 1)) | ((z == planes - 1) & (p == 0))
        return (
            (up, column_copy(index, o_up_s.at[p], me + SEQS)),
            (down, column_copy(index, o_dn_s.at[p], me - SEQS)),
            (keep & ends, column_copy(index, o_far_s, at_x, "groups")),
            (c == group, column_copy(index, o_y_s.at[p], at_y)),
            (None, column_copy(index, o_c_s.at[p * 2 + y], at_core)),
        )

    def column_seconds(p):
        index = p * SEQS + (1 - y) * 2 + c
        return (
            column_copy(index, o_x_s.at[p], at_x, "groups"),
            column_copy(index, o_c_s.at[p * 2 + 1 - y], at_core),
        )

    def start_all(copies):
        for condition, copy in copies:
            if condition is None:
                copy.start()
            else:
                pl.when(condition)(copy.start)

    def sent_all(copies):
        for condition, copy in copies:
            if condition is None:
                copy.wait_send()
            else:
                pl.when(condition)(copy.wait_send)

    start_all(column_forwards(z))
    for by in range(1, planes):
        plane = lax.rem(z + by, planes)
        kv_copy(plane, by).wait_recv()
        put(
            table(column, plane, 1), table(column, plane, 1), t_s.at[by], t_r.at[plane], at_y
        ).wait_recv()
    tables_to_y().start()

    total_keys = planes * n
    lane = lax.broadcasted_iota(jnp.int32, (n, total_keys), 1)
    key_plane = lane // n
    key_position = lane % n
    for plane in range(planes):
        key_position = key_position + jnp.where(
            key_plane == plane, order_ref[plane * SEQS + place] * n, 0
        )
    query_position = order_ref[me] * n + lax.broadcasted_iota(jnp.int32, (n, total_keys), 0)
    visible = key_position <= query_position
    heads = width // HEAD_SIZE
    kv_heads = kv_width // HEAD_SIZE

    def attend(head, carry):
        cols = pl.ds(pl.multiple_of(head * HEAD_SIZE, HEAD_SIZE), HEAD_SIZE)
        kv_head = head // (heads // kv_heads)
        key_cols = pl.ds(pl.multiple_of(kv_head * HEAD_SIZE, HEAD_SIZE), HEAD_SIZE)
        value_cols = pl.ds(pl.multiple_of(kv_width + kv_head * HEAD_SIZE, HEAD_SIZE), HEAD_SIZE)
        scores = lax.dot_general(
            queries_ref[:, cols],
            kv[:, key_cols],
            (((1,), (1,)), ((), ())),
            preferred_element_type=jnp.float32,
        ) * (HEAD_SIZE**-0.5)
        scores = jnp.where(visible, scores, -jnp.inf)
        weights = jnp.exp(scores - jnp.max(scores, axis=1, keepdims=True))
        total = jnp.sum(weights, axis=1, keepdims=True)
        summed = jnp.dot(
            weights.astype(jnp.bfloat16), kv[:, value_cols], preferred_element_type=jnp.float32
        )
        context_ref[:, cols] = (summed / total).astype(jnp.bfloat16)
        return carry

    lax.fori_loop(0, heads, attend, 0, unroll=4)
    tables_to_y().wait_recv()
    tables_to_core().start()

    def weight_step(k, carry):
        @pl.when(k < planes)
        def _():
            p = plane_at(k, z, planes)
            column_copy(p * SEQS + place, o_y_s.at[p], at_y).wait_recv()
            start_all(column_forwards(p))

        @pl.when((k <= planes) & (c == group))
        def _():
            p = plane_at(k - 1, z, planes)
            column_copy(p * SEQS + (1 - y) * 2 + c, o_y_s.at[p], at_y).wait_recv()
            for copy in column_seconds(p):
                copy.start()

        @pl.when(k > 1)
        def _():
            p = plane_at(k - 2, z, planes)

            @pl.when(c != group)
            def _():
                column_copy(p * SEQS + (1 - y) * 2 + c, o_y_s.at[p], at_y).wait_recv()
                column_seconds(p)[1].start()

            for row in range(2):
                column_copy(p * SEQS + row * 2 + 1 - c, o_y_s.at[p], at_core).wait_recv()
            for spot in range(SEQS):
                index = p * SEQS + spot
                each = columns.shape[2]
                cols = pl.ds(pl.multiple_of(index * each, each), each)
                updated_ref[:, cols] = residual_ref[:, cols].astype(jnp.float32) + jnp.dot(
                    context_ref[...], columns[index], preferred_element_type=jnp.float32
                )

        return carry

    lax.fori_loop(1, planes + 2, weight_step, 0)
    tables_to_core().wait_recv()

    def norm(i, carry):
        rows = pl.ds(pl.multiple_of(i * 16, 16), 16)
        rows_there = pl.ds(pl.multiple_of(me * n + i * 16, 16), 16)
        updated = updated_ref[rows, :]
        mean = jnp.mean(updated * updated, axis=1, keepdims=True)
        rows_all[rows_there, :] = (updated * lax.rsqrt(mean + 1e-06) * gain_ref[...]).astype(
            jnp.bfloat16
        )
        return carry

    lax.fori_loop(0, n // 16, norm, 0)
    for p in range(planes):
        for row in range(2):
            for core in range(2):
                at = ((core * 2 + row) * planes + p) * experts + me
                gates_ref[pl.ds(p * 2 + row, 1), pl.ds(core * n, n)] = tables[pl.ds(at, 1), :]

    def gather_copy(index, sem, to):
        return put(block(rows_all, index), block(rows_all, index), sem, recv.at[index], to)

    def forwards(p):
        index = p * SEQS + place
        return (
            (above & (p <= z), gather_copy(index, up_s.at[p], me + SEQS)),
            (below & (p >= z), gather_copy(index, dn_s.at[p], me - SEQS)),
            (None, gather_copy(index, y_s.at[p], at_y)),
            (None, gather_copy(index, c_s.at[p * 2 + y], at_core)),
        )

    def second_forward(p):
        return gather_copy(p * SEQS + (1 - y) * 2 + c, c_s.at[p * 2 + 1 - y], at_core)

    def core_return(p, row):
        return put(
            block(contrib, p * SEQS + row * 2 + 1 - c),
            block(from_core, p * 2 + row),
            rc_s.at[p * 2 + row],
            rc_r.at[p * 2 + row],
            at_core,
        )

    small = n // HALVES

    def piece(ref, index, h):
        return ref.at[pl.ds(pl.multiple_of(index * n + h * small, small), small)]

    def y_return(p, h):
        at = p * HALVES + h
        return put(
            piece(contrib, p * SEQS + (1 - y) * 2 + c, h),
            piece(from_y, p, h),
            ry_s.at[at],
            ry_r.at[at],
            at_y,
        )

    def z_return(p, slot, h, to):
        return put(
            piece(contrib, p * SEQS + place, h),
            piece(from_z, slot, h),
            rz_s.at[p * HALVES + h],
            rz_r.at[slot * HALVES + h],
            to,
        )

    shape = (pair, pair)
    earlier = lax.broadcasted_iota(jnp.int32, shape, 0)
    later = lax.broadcasted_iota(jnp.int32, shape, 1)
    before = (earlier < later) & (earlier // n == later // n)
    routed = gates_ref[...] > 0
    count = jnp.dot(
        routed.astype(jnp.bfloat16), before.astype(jnp.bfloat16), preferred_element_type=jnp.float32
    ).astype(jnp.int32)
    offset = lax.broadcasted_iota(jnp.int32, count.shape, 1) // n * cap
    ranks[...] = jnp.where(routed, count + offset, -1)

    def compute(p):
        parts = []
        for half in range(2):
            row = pl.ds(p * 2 + half, 1)
            hit = lax.broadcasted_iota(jnp.int32, (2 * cap, pair), 0) == ranks[row, :]
            gate = jnp.sum(jnp.where(hit, gates_ref[row, :], 0.0), axis=1, keepdims=True)
            chosen = hit.astype(jnp.float32)
            parts.append((chosen.astype(jnp.bfloat16), chosen.T.astype(jnp.bfloat16), gate))
        tile = 512

        def pick(j, carry):
            cols = pl.ds(pl.multiple_of(j * tile, tile), tile)
            for half in range(2):
                source = pl.ds(pl.multiple_of((p * 2 + half) * pair, pair), pair)
                picked[pl.ds(half * 2 * cap, 2 * cap), cols] = jnp.dot(
                    parts[half][0], rows_all[source, cols], preferred_element_type=jnp.float32
                ).astype(jnp.bfloat16)
            return carry

        lax.fori_loop(0, width // tile, pick, 0, unroll=2)
        narrow = 256

        def gate_up(j, carry):
            first = pl.ds(pl.multiple_of(j * narrow, narrow), narrow)
            second = pl.ds(pl.multiple_of(hidden + j * narrow, narrow), narrow)
            v = jnp.dot(picked[...], w_up[:, first], preferred_element_type=jnp.float32)
            u = jnp.dot(picked[...], w_up[:, second], preferred_element_type=jnp.float32)
            act[:, first] = (v / (1.0 + jnp.exp(-v)) * u).astype(jnp.bfloat16)
            return carry

        lax.fori_loop(0, hidden // narrow, gate_up, 0)

        def down(j, carry):
            cols = pl.ds(pl.multiple_of(j * tile, tile), tile)
            result = jnp.dot(act[...], w_down[:, cols], preferred_element_type=jnp.float32)
            for half in range(2):
                unused, spread_back, gate = parts[half]
                source = pl.ds(pl.multiple_of((p * 2 + half) * pair, pair), pair)
                part = result[half * 2 * cap : (half + 1) * 2 * cap] * gate
                contrib[source, cols] = jnp.dot(
                    spread_back, part.astype(jnp.bfloat16), preferred_element_type=jnp.float32
                ).astype(jnp.bfloat16)
            return carry

        lax.fori_loop(0, width // tile, down, 0, unroll=2)

    chunk = 16

    def add_up(target, terms):
        def some(i, carry):
            here = pl.ds(pl.multiple_of(i * chunk, chunk), chunk)
            total = terms[0][here, :].astype(jnp.float32)
            for term in terms[1:]:
                total = total + term[here, :].astype(jnp.float32)
            target[here, :] = total.astype(target.dtype)
            return carry

        lax.fori_loop(0, small // chunk, some, 0)

    def core_sum(p):
        for row in range(2):
            core_return(p, row).wait_recv()
        for h in range(HALVES):
            other = piece(contrib, p * SEQS + (1 - y) * 2 + c, h)
            add_up(other, [other, piece(from_core, p * 2 + 1 - y, h)])
            y_return(p, h).start()

    def advance(k, carry):
        @pl.when(k < planes)
        def _():
            p = plane_at(k, z, planes)

            @pl.when(k > 0)
            def _():
                gather_copy(p * SEQS + place, y_s.at[p], at_y).wait_recv()

            start_all(forwards(p))

        j = k - lag

        @pl.when((j >= 0) & (j < planes))
        def _():
            p = plane_at(j, z, planes)
            second_forward(p).wait_recv()
            second_forward(p).start()
            pl.when(j == planes - 1)(lambda: core_sum(z))
            for row in range(2):
                gather_copy(p * SEQS + row * 2 + 1 - c, c_s.at[0], at_core).wait_recv()

            @pl.when(j == 0)
            def _():
                load_up.wait()
                load_down.wait()

            compute(p)
            for row in range(2):
                core_return(p, row).start()

        return carry

    lag = 1 + jnp.where(above & below, 1, 0)
    lax.fori_loop(0, planes + 2, advance, 0)
    def far_sum(i, carry):
        core_sum(plane_at(planes - 1 - i, z, planes))
        return carry

    lax.fori_loop(0, planes - 1, far_sum, 0)

    def chain(i, carry):
        p = plane_at(planes - 1 - i // HALVES, z, planes)
        h = i % HALVES
        y_return(p, h).wait_recv()
        own = piece(contrib, p * SEQS + place, h)
        terms = [own, piece(from_core, p * 2 + y, h), piece(from_y, p, h)]
        onward = ((p < z) & above) | ((p > z) & below)

        @pl.when(onward)
        def _():
            z_return(p, p, h, at_y).wait_recv()
            add_up(own, terms + [piece(from_z, p, h)])

        pl.when(jnp.logical_not(onward))(lambda: add_up(own, terms))

        @pl.when(p < z)
        def _():
            z_return(p, jnp.where(p == z - 1, planes, p), h, me - SEQS).start()

        @pl.when(p > z)
        def _():
            z_return(p, p, h, me + SEQS).start()

        return carry

    lax.fori_loop(0, (planes - 1) * HALVES, chain, 0)

    def last(h, carry):
        y_return(z, h).wait_recv()
        result = piece(out_ref, 0, h)
        terms = [
            piece(updated_ref, 0, h),
            piece(contrib, me, h),
            piece(from_core, z * 2 + y, h),
            piece(from_y, z, h),
        ]
        low, high = piece(from_z, z, h), piece(from_z, planes, h)
        pl.when(below)(lambda: z_return(z, z, h, at_y).wait_recv())
        pl.when(above)(lambda: z_return(z, planes, h, at_y).wait_recv())
        pl.when(below & above)(lambda: add_up(result, terms + [low, high]))
        pl.when(below & jnp.logical_not(above))(lambda: add_up(result, terms + [low]))
        pl.when(jnp.logical_not(below) & above)(lambda: add_up(result, terms + [high]))
        return carry

    lax.fori_loop(0, HALVES, last, 0)

    for by in range(1, planes):
        for copy in send_kv(by):
            copy.wait_send()
    tables_to_y().wait_send()
    tables_to_core().wait_send()

    def finish(p, carry):
        sent_all(column_forwards(p))
        pl.when(c == group)(column_seconds(p)[0].wait_send)
        column_seconds(p)[1].wait_send()
        sent_all(forwards(p))
        second_forward(p).wait_send()
        for row in range(2):
            core_return(p, row).wait_send()
        for h in range(HALVES):
            y_return(p, h).wait_send()

        @pl.when(p != z)
        def _():
            for h in range(HALVES):
                z_return(p, p, h, at_y).wait_send()

        return carry

    lax.fori_loop(0, planes, finish, 0)


def layer_call(
    order,
    residual,
    queries,
    keys,
    values,
    choices,
    gain,
    out_weight,
    w_gate_up,
    w_down,
    cap,
):
    n, width = residual.shape
    hidden = w_down.shape[1]
    devices = lax.axis_size("ctx")
    planes = devices // SEQS
    vmem = pl.BlockSpec(memory_space=pltpu.VMEM)
    anywhere = pl.BlockSpec(memory_space=pl.ANY)
    bf16 = jnp.bfloat16
    dma = pltpu.SemaphoreType.DMA
    return pl.pallas_call(
        functools.partial(layer_kernel, planes, cap),
        out_shape=[jax.ShapeDtypeStruct((n, width), bf16)] * 2,
        in_specs=[pl.BlockSpec(memory_space=pltpu.SMEM)] + [vmem] * 7 + [anywhere] * 2,
        out_specs=[vmem, vmem],
        scratch_shapes=[
            pltpu.VMEM((planes * n, 2 * keys.shape[1]), bf16),
            pltpu.VMEM((devices * devices, n), jnp.float32),
            pltpu.VMEM((2 * planes, 2 * n), jnp.float32),
            pltpu.VMEM((devices,) + out_weight.shape, bf16),
            pltpu.VMEM((n, width), jnp.float32),
            pltpu.VMEM((devices * n, width), bf16),
            pltpu.VMEM((devices * n, width), bf16),
            pltpu.VMEM((2 * planes * n, width), bf16),
            pltpu.VMEM((planes * n, width), bf16),
            pltpu.VMEM(((planes + 1) * n, width), bf16),
            pltpu.VMEM(w_gate_up.shape[1:], bf16),
            pltpu.VMEM(w_down.shape[1:], bf16),
            pltpu.VMEM((2 * planes, 2 * n), jnp.int32),
            pltpu.VMEM((SEQS * cap, width), bf16),
            pltpu.VMEM((SEQS * cap, hidden), bf16),
            dma((planes,)),
            dma((planes,)),
            dma((planes + 2,)),
            dma((planes + 2,)),
            dma((devices,)),
            dma((planes,)),
            dma((planes,)),
            dma((planes,)),
            dma((planes,)),
            dma((2 * planes,)),
            dma,
            dma((2,)),
            dma((devices,)),
            dma((planes,)),
            dma((planes,)),
            dma((planes,)),
            dma((2 * planes,)),
            dma((2 * planes,)),
            dma((2 * planes,)),
            dma((HALVES * planes,)),
            dma((HALVES * planes,)),
            dma((HALVES * planes,)),
            dma((HALVES * (planes + 1),)),
        ],
        compiler_params=pltpu.CompilerParams(
            collective_id=0, has_side_effects=True, vmem_limit_bytes=VMEM_BYTES
        ),
        name="layer",
    )(order, residual, queries, keys, values, choices, gain, out_weight, w_gate_up, w_down)


def fits(devices, rows, width, hidden):
    blocks = 4 * devices + 8
    return lax.axis_size("groups") == 2 and 2 * (blocks * rows * width + 3 * width * hidden) < VMEM_BYTES * 4 // 5


def local(
    residual,
    queries,
    keys,
    values,
    block_order,
    routes,
    route_weights,
    out_weight,
    norm_gain,
    w_gate_up,
    w_down,
):
    device_row_count = queries.shape[0]
    query_group_width = QUERY_HEADS // KEY_VALUE_HEADS
    devices = lax.axis_size("ctx")
    cycle_length = devices // SEQS
    own_index = lax.axis_index("ctx")
    experts = devices * w_gate_up.shape[0]
    capacity = 9 * device_row_count * TOPK // (8 * experts)
    if fits(devices, device_row_count, D, FF):
        return tuple(
            layer_call(
                block_order,
                residual,
                queries,
                keys,
                values,
                jnp.concatenate([routes.astype(jnp.float32), route_weights], axis=1),
                norm_gain.reshape(1, -1),
                out_weight,
                w_gate_up,
                w_down,
                capacity,
            )
        )
    full_weight = lax.all_gather(out_weight, "ctx", axis=1, tiled=True)
    query_position = block_order[own_index]
    query_head_rows = (
        queries.reshape(device_row_count, KEY_VALUE_HEADS, query_group_width, HEAD_SIZE)
        .transpose(1, 2, 0, 3)
        .reshape(KEY_VALUE_HEADS, query_group_width * device_row_count, HEAD_SIZE)
    )
    query_offset = jnp.arange(query_group_width * device_row_count) % device_row_count
    key_offset = jnp.arange(device_row_count)
    scale = HEAD_SIZE ** (-0.5)

    def update(carry, key_value_tuple, key_position):
        summed, running_max, totals = carry
        local_key_block = key_value_tuple[0].reshape(device_row_count, KEY_VALUE_HEADS, HEAD_SIZE)
        local_value_block = key_value_tuple[1].reshape(device_row_count, KEY_VALUE_HEADS, HEAD_SIZE)
        scores = (
            jnp.einsum(
                "hqd,khd->hqk", query_head_rows, local_key_block, preferred_element_type=jnp.float32
            )
            * scale
        )
        visible = (
            key_position * device_row_count + key_offset[None, :]
            <= query_position * device_row_count + query_offset[:, None]
        )
        scores = jnp.where(visible[None], scores, -jnp.inf)
        new_max = jnp.maximum(running_max, jnp.max(scores, axis=-1))
        factor = jnp.exp(running_max - new_max)
        weights = jnp.exp(scores - new_max[..., None])
        totals = totals * factor + jnp.sum(weights, axis=-1)
        summed = summed * factor[..., None] + jnp.einsum(
            "hqk,khd->hqd",
            weights.astype(jnp.bfloat16),
            local_value_block,
            preferred_element_type=jnp.float32,
        )
        return (summed, new_max, totals)

    initial = (
        jnp.zeros((KEY_VALUE_HEADS, query_group_width * device_row_count, HEAD_SIZE), jnp.float32),
        jnp.full((KEY_VALUE_HEADS, query_group_width * device_row_count), -jnp.inf, jnp.float32),
        jnp.zeros((KEY_VALUE_HEADS, query_group_width * device_row_count), jnp.float32),
    )
    local_pair = jnp.stack([keys, values])
    carry = update(initial, local_pair, query_position)

    def advance(step, state):
        current, moving = state
        moving = shifted(moving, "ctx", SEQS)
        anchor = jnp.mod(own_index - SEQS * step, devices)
        key_position = block_order[anchor]
        current = lax.cond(
            key_position <= query_position,
            lambda inner: update(inner, moving, key_position),
            lambda inner: inner,
            current,
        )
        return (current, moving)

    carry, passed = lax.fori_loop(1, cycle_length, advance, (carry, local_pair))
    summed, running_max, totals = carry
    context = (
        (summed / totals[..., None])
        .reshape(KEY_VALUE_HEADS, query_group_width, device_row_count, HEAD_SIZE)
        .transpose(2, 0, 1, 3)
        .reshape(device_row_count, QUERY_HEADS * HEAD_SIZE)
        .astype(jnp.bfloat16)
    )
    projected = jnp.dot(context, full_weight, preferred_element_type=jnp.float32)
    updated = residual.astype(jnp.float32) + projected
    normed = (
        updated * lax.rsqrt(jnp.mean(updated * updated, axis=-1, keepdims=True) + 1e-06) * norm_gain
    ).astype(jnp.bfloat16)
    experts = devices * w_gate_up.shape[0]
    capacity = 9 * device_row_count * TOPK // (8 * experts)
    expert_ids = routes.reshape(-1)
    one_hot = (expert_ids[:, None] == jnp.arange(experts, dtype=jnp.int32)[None, :]).astype(
        jnp.int32
    )
    ranks = jnp.sum(jnp.cumsum(one_hot, axis=0) * one_hot, axis=1) - 1
    target = expert_ids * capacity + ranks
    source_row = jnp.arange(device_row_count * TOPK) // TOPK
    outgoing = (
        jnp.zeros((experts * capacity, D), jnp.bfloat16)
        .at[target]
        .set(normed[source_row])
        .reshape(experts, capacity, D)
    )
    arrived = lax.all_to_all(outgoing, "ctx", split_axis=0, concat_axis=0, tiled=True)
    flat = arrived.reshape(-1, D)
    both = jnp.dot(flat, w_gate_up[0], preferred_element_type=jnp.float32)
    hidden = (jax.nn.silu(both[:, :FF]) * both[:, FF:]).astype(jnp.bfloat16)
    result = (
        jnp.dot(hidden, w_down[0], preferred_element_type=jnp.float32)
        .astype(jnp.bfloat16)
        .reshape(arrived.shape)
    )
    returned = lax.all_to_all(result, "ctx", split_axis=0, concat_axis=0, tiled=True)
    gathered = returned.reshape(-1, D)[target].reshape(device_row_count, TOPK, D)
    gates = route_weights / jnp.sum(route_weights, axis=-1, keepdims=True)
    mixed = updated
    for slot in range(TOPK):
        mixed = mixed + gates[:, slot : slot + 1] * gathered[:, slot].astype(jnp.float32)
    return (context, mixed.astype(jnp.bfloat16))


def solution(mesh):
    placed = (
        P(("groups", "ctx"), None),
        P(("groups", "ctx"), None),
        P(("groups", "ctx"), None),
        P(("groups", "ctx"), None),
        P("groups"),
        P(("groups", "ctx"), None),
        P(("groups", "ctx"), None),
        P(None, "ctx"),
        P(),
        P("ctx", None, None),
        P("ctx", None, None),
    )
    return jax.shard_map(
        local,
        mesh=mesh,
        in_specs=placed,
        out_specs=(P(("groups", "ctx"), None), P(("groups", "ctx"), None)),
        check_vma=False,
    )
```

```python
import functools

import jax
import jax.numpy as jnp
from jax import lax
from jax.experimental import pallas as pl
from jax.experimental.pallas import tpu as pltpu
from jax.sharding import PartitionSpec as P

D = 2048
HEAD_SIZE = 128
FF = 768
QUERY_HEADS = 16
KEY_VALUE_HEADS = 2
TOPK = 8
SEQS = 4


def shifted(array, axis, by):
    devices = lax.axis_size(axis)
    return lax.ppermute(array, axis, [(i, (i + by) % devices) for i in range(devices)])


VMEM_BYTES = 60 * 2**20
HALVES = 4


def put(src, dst, send_sem, recv_sem, to, axis="ctx"):
    return pltpu.make_async_remote_copy(
        src_ref=src,
        dst_ref=dst,
        send_sem=send_sem,
        recv_sem=recv_sem,
        device_id={axis: to},
        device_id_type=pl.DeviceIdType.MESH,
    )


def plane_at(step, z, planes):
    short = jnp.minimum(z, planes - 1 - z)
    sign = jnp.where(2 * z < planes - 1, 1, -1)
    near = (step + 1) // 2 * (2 * (step % 2) - 1)
    return z + sign * jnp.where(step <= 2 * short, near, step - short)


def layer_kernel(
    planes,
    cap,
    order_ref,
    residual_ref,
    queries_ref,
    keys_ref,
    values_ref,
    choices_ref,
    gain_ref,
    weight_ref,
    up_hbm,
    down_hbm,
    context_ref,
    out_ref,
    kv,
    tables,
    gates_ref,
    columns,
    updated_ref,
    rows_all,
    contrib,
    from_core,
    from_y,
    from_z,
    w_up,
    w_down,
    ranks,
    picked,
    act,
    kv_s,
    kv_r,
    t_s,
    t_r,
    o_recv,
    o_up_s,
    o_dn_s,
    o_y_s,
    o_x_s,
    o_c_s,
    o_far_s,
    w_sem,
    recv,
    up_s,
    dn_s,
    y_s,
    c_s,
    rc_s,
    rc_r,
    ry_s,
    ry_r,
    rz_s,
    rz_r,
):
    n, width = residual_ref.shape
    hidden = w_down.shape[0]
    pair = 2 * n
    me = lax.axis_index("ctx")
    z, place = me // SEQS, me % SEQS
    y, c = place // 2, place % 2
    at_y = z * SEQS + (1 - y) * 2 + c
    at_core = z * SEQS + y * 2 + (1 - c)
    above, below = z < planes - 1, z > 0

    def block(ref, index):
        return ref.at[pl.ds(pl.multiple_of(index * n, n), n)]

    load_up = pltpu.make_async_copy(up_hbm.at[0], w_up, w_sem.at[0])
    load_down = pltpu.make_async_copy(down_hbm.at[0], w_down, w_sem.at[1])
    load_up.start()
    load_down.start()

    barrier = pltpu.get_barrier_semaphore()

    def greet(to, axis="ctx"):
        pl.semaphore_signal(
            barrier, inc=1, device_id={axis: to}, device_id_type=pl.DeviceIdType.MESH
        )

    group = lax.axis_index("groups")
    at_x = 1 - group
    experts = planes * SEQS
    greet(at_x, "groups")
    greet(at_y)
    greet(at_core)
    for by in range(1, planes):
        greet(lax.rem(z + by, planes) * SEQS + place)
    kv_width = keys_ref.shape[1]
    own_kv = block(kv, z)
    own_kv[:, :kv_width] = keys_ref[...]
    own_kv[:, kv_width:] = values_ref[...]
    column = c * 2 + y

    def table(col, plane, count):
        start = pl.multiple_of((col * planes + plane) * experts, experts)
        return tables.at[pl.ds(start, count * experts)]

    slots = choices_ref.shape[1] // 2
    routes, shares = choices_ref[:, :slots], choices_ref[:, slots:]
    gates = shares / jnp.sum(shares, axis=1, keepdims=True)
    expert_lane = lax.broadcasted_iota(jnp.int32, (n, HEAD_SIZE), 1).astype(jnp.float32)
    spread = jnp.zeros((n, HEAD_SIZE), jnp.float32)
    for slot in range(slots):
        spread = spread + jnp.where(
            routes[:, slot : slot + 1] == expert_lane, gates[:, slot : slot + 1], 0.0
        )
    table(column, z, 1)[...] = spread.T[:experts]
    columns[me] = weight_ref[...]
    pl.semaphore_wait(barrier, planes + 2)

    def kv_copy(plane, by):
        return put(block(kv, plane), block(kv, plane), kv_s.at[by], kv_r.at[plane], at_y)

    def send_kv(by):
        to = lax.rem(z + by, planes) * SEQS + place
        return (
            put(own_kv, own_kv, kv_s.at[by], kv_r.at[z], to),
            put(table(column, z, 1), table(column, z, 1), t_s.at[by], t_r.at[z], to),
        )

    def tables_to_y():
        part = table(column, 0, planes)
        return put(part, part, t_s.at[planes], t_r.at[planes], at_y)

    def tables_to_core():
        part = table(c * 2, 0, 2 * planes)
        return put(part, part, t_s.at[planes + 1], t_r.at[planes + 1], at_core)

    for by in range(1, planes):
        for copy in send_kv(by):
            copy.start()

    def column_copy(index, sem, to, axis="ctx"):
        return put(columns.at[index], columns.at[index], sem, o_recv.at[index], to, axis)

    def column_forwards(p):
        index = p * SEQS + place
        keep = c == group
        up = above & (p <= z) & (keep | (p > 0) | (z + 2 < planes))
        down = below & (p >= z) & (keep | (p < planes - 1) | (z > 1))
        ends = ((z == 0) & (p == planes - 1)) | ((z == planes - 1) & (p == 0))
        return (
            (up, column_copy(index, o_up_s.at[p], me + SEQS)),
            (down, column_copy(index, o_dn_s.at[p], me - SEQS)),
            (keep & ends, column_copy(index, o_far_s, at_x, "groups")),
            (c == group, column_copy(index, o_y_s.at[p], at_y)),
            (None, column_copy(index, o_c_s.at[p * 2 + y], at_core)),
        )

    def column_seconds(p):
        index = p * SEQS + (1 - y) * 2 + c
        return (
            column_copy(index, o_x_s.at[p], at_x, "groups"),
            column_copy(index, o_c_s.at[p * 2 + 1 - y], at_core),
        )

    def start_all(copies):
        for condition, copy in copies:
            if condition is None:
                copy.start()
            else:
                pl.when(condition)(copy.start)

    def sent_all(copies):
        for condition, copy in copies:
            if condition is None:
                copy.wait_send()
            else:
                pl.when(condition)(copy.wait_send)

    start_all(column_forwards(z))
    for by in range(1, planes):
        plane = lax.rem(z + by, planes)
        kv_copy(plane, by).wait_recv()
        put(
            table(column, plane, 1), table(column, plane, 1), t_s.at[by], t_r.at[plane], at_y
        ).wait_recv()
    tables_to_y().start()

    total_keys = planes * n
    lane = lax.broadcasted_iota(jnp.int32, (n, total_keys), 1)
    key_plane = lane // n
    key_position = lane % n
    for plane in range(planes):
        key_position = key_position + jnp.where(
            key_plane == plane, order_ref[plane * SEQS + place] * n, 0
        )
    query_position = order_ref[me] * n + lax.broadcasted_iota(jnp.int32, (n, total_keys), 0)
    visible = key_position <= query_position
    heads = width // HEAD_SIZE
    kv_heads = kv_width // HEAD_SIZE

    def attend(head, carry):
        cols = pl.ds(pl.multiple_of(head * HEAD_SIZE, HEAD_SIZE), HEAD_SIZE)
        kv_head = head // (heads // kv_heads)
        key_cols = pl.ds(pl.multiple_of(kv_head * HEAD_SIZE, HEAD_SIZE), HEAD_SIZE)
        value_cols = pl.ds(pl.multiple_of(kv_width + kv_head * HEAD_SIZE, HEAD_SIZE), HEAD_SIZE)
        scores = lax.dot_general(
            queries_ref[:, cols],
            kv[:, key_cols],
            (((1,), (1,)), ((), ())),
            preferred_element_type=jnp.float32,
        ) * (HEAD_SIZE**-0.5)
        scores = jnp.where(visible, scores, -jnp.inf)
        weights = jnp.exp(scores - jnp.max(scores, axis=1, keepdims=True))
        total = jnp.sum(weights, axis=1, keepdims=True)
        summed = jnp.dot(
            weights.astype(jnp.bfloat16), kv[:, value_cols], preferred_element_type=jnp.float32
        )
        context_ref[:, cols] = (summed / total).astype(jnp.bfloat16)
        return carry

    lax.fori_loop(0, heads, attend, 0, unroll=4)
    tables_to_y().wait_recv()
    tables_to_core().start()

    def weight_step(k, carry):
        @pl.when(k < planes)
        def _():
            p = plane_at(k, z, planes)
            column_copy(p * SEQS + place, o_y_s.at[p], at_y).wait_recv()
            start_all(column_forwards(p))

        @pl.when((k <= planes) & (c == group))
        def _():
            p = plane_at(k - 1, z, planes)
            column_copy(p * SEQS + (1 - y) * 2 + c, o_y_s.at[p], at_y).wait_recv()
            for copy in column_seconds(p):
                copy.start()

        @pl.when(k > 1)
        def _():
            p = plane_at(k - 2, z, planes)

            @pl.when(c != group)
            def _():
                column_copy(p * SEQS + (1 - y) * 2 + c, o_y_s.at[p], at_y).wait_recv()
                column_seconds(p)[1].start()

            for row in range(2):
                column_copy(p * SEQS + row * 2 + 1 - c, o_y_s.at[p], at_core).wait_recv()
            for spot in range(SEQS):
                index = p * SEQS + spot
                each = columns.shape[2]
                cols = pl.ds(pl.multiple_of(index * each, each), each)
                updated_ref[:, cols] = residual_ref[:, cols].astype(jnp.float32) + jnp.dot(
                    context_ref[...], columns[index], preferred_element_type=jnp.float32
                )

        return carry

    lax.fori_loop(1, planes + 2, weight_step, 0)
    tables_to_core().wait_recv()

    def norm(i, carry):
        rows = pl.ds(pl.multiple_of(i * 16, 16), 16)
        rows_there = pl.ds(pl.multiple_of(me * n + i * 16, 16), 16)
        updated = updated_ref[rows, :]
        mean = jnp.mean(updated * updated, axis=1, keepdims=True)
        rows_all[rows_there, :] = (updated * lax.rsqrt(mean + 1e-06) * gain_ref[...]).astype(
            jnp.bfloat16
        )
        return carry

    lax.fori_loop(0, n // 16, norm, 0)
    for p in range(planes):
        for row in range(2):
            for core in range(2):
                at = ((core * 2 + row) * planes + p) * experts + me
                gates_ref[pl.ds(p * 2 + row, 1), pl.ds(core * n, n)] = tables[pl.ds(at, 1), :]

    def gather_copy(index, sem, to):
        return put(block(rows_all, index), block(rows_all, index), sem, recv.at[index], to)

    def forwards(p):
        index = p * SEQS + place
        return (
            (above & (p <= z), gather_copy(index, up_s.at[p], me + SEQS)),
            (below & (p >= z), gather_copy(index, dn_s.at[p], me - SEQS)),
            (None, gather_copy(index, y_s.at[p], at_y)),
            (None, gather_copy(index, c_s.at[p * 2 + y], at_core)),
        )

    def second_forward(p):
        return gather_copy(p * SEQS + (1 - y) * 2 + c, c_s.at[p * 2 + 1 - y], at_core)

    def core_return(p, row):
        return put(
            block(contrib, p * SEQS + row * 2 + 1 - c),
            block(from_core, p * 2 + row),
            rc_s.at[p * 2 + row],
            rc_r.at[p * 2 + row],
            at_core,
        )

    small = n // HALVES

    def piece(ref, index, h):
        return ref.at[pl.ds(pl.multiple_of(index * n + h * small, small), small)]

    def y_return(p, h):
        at = p * HALVES + h
        return put(
            piece(contrib, p * SEQS + (1 - y) * 2 + c, h),
            piece(from_y, p, h),
            ry_s.at[at],
            ry_r.at[at],
            at_y,
        )

    def z_return(p, slot, h, to):
        return put(
            piece(contrib, p * SEQS + place, h),
            piece(from_z, slot, h),
            rz_s.at[p * HALVES + h],
            rz_r.at[slot * HALVES + h],
            to,
        )

    shape = (pair, pair)
    earlier = lax.broadcasted_iota(jnp.int32, shape, 0)
    later = lax.broadcasted_iota(jnp.int32, shape, 1)
    before = (earlier < later) & (earlier // n == later // n)
    routed = gates_ref[...] > 0
    count = jnp.dot(
        routed.astype(jnp.bfloat16), before.astype(jnp.bfloat16), preferred_element_type=jnp.float32
    ).astype(jnp.int32)
    offset = lax.broadcasted_iota(jnp.int32, count.shape, 1) // n * cap
    ranks[...] = jnp.where(routed, count + offset, -1)

    def compute(p):
        parts = []
        for half in range(2):
            row = pl.ds(p * 2 + half, 1)
            hit = lax.broadcasted_iota(jnp.int32, (2 * cap, pair), 0) == ranks[row, :]
            gate = jnp.sum(jnp.where(hit, gates_ref[row, :], 0.0), axis=1, keepdims=True)
            chosen = hit.astype(jnp.float32)
            parts.append((chosen.astype(jnp.bfloat16), chosen.T.astype(jnp.bfloat16), gate))
        tile = 512

        def pick(j, carry):
            cols = pl.ds(pl.multiple_of(j * tile, tile), tile)
            for half in range(2):
                source = pl.ds(pl.multiple_of((p * 2 + half) * pair, pair), pair)
                picked[pl.ds(half * 2 * cap, 2 * cap), cols] = jnp.dot(
                    parts[half][0], rows_all[source, cols], preferred_element_type=jnp.float32
                ).astype(jnp.bfloat16)
            return carry

        lax.fori_loop(0, width // tile, pick, 0, unroll=2)
        narrow = 256

        def gate_up(j, carry):
            first = pl.ds(pl.multiple_of(j * narrow, narrow), narrow)
            second = pl.ds(pl.multiple_of(hidden + j * narrow, narrow), narrow)
            v = jnp.dot(picked[...], w_up[:, first], preferred_element_type=jnp.float32)
            u = jnp.dot(picked[...], w_up[:, second], preferred_element_type=jnp.float32)
            act[:, first] = (v / (1.0 + jnp.exp(-v)) * u).astype(jnp.bfloat16)
            return carry

        lax.fori_loop(0, hidden // narrow, gate_up, 0)

        def down(j, carry):
            cols = pl.ds(pl.multiple_of(j * tile, tile), tile)
            result = jnp.dot(act[...], w_down[:, cols], preferred_element_type=jnp.float32)
            for half in range(2):
                unused, spread_back, gate = parts[half]
                source = pl.ds(pl.multiple_of((p * 2 + half) * pair, pair), pair)
                part = result[half * 2 * cap : (half + 1) * 2 * cap] * gate
                contrib[source, cols] = jnp.dot(
                    spread_back, part.astype(jnp.bfloat16), preferred_element_type=jnp.float32
                ).astype(jnp.bfloat16)
            return carry

        lax.fori_loop(0, width // tile, down, 0, unroll=2)

    chunk = 16

    def add_up(target, terms):
        def some(i, carry):
            here = pl.ds(pl.multiple_of(i * chunk, chunk), chunk)
            total = terms[0][here, :].astype(jnp.float32)
            for term in terms[1:]:
                total = total + term[here, :].astype(jnp.float32)
            target[here, :] = total.astype(target.dtype)
            return carry

        lax.fori_loop(0, small // chunk, some, 0)

    def core_sum(p):
        for row in range(2):
            core_return(p, row).wait_recv()
        for h in range(HALVES):
            other = piece(contrib, p * SEQS + (1 - y) * 2 + c, h)
            add_up(other, [other, piece(from_core, p * 2 + 1 - y, h)])
            y_return(p, h).start()

    def advance(k, carry):
        @pl.when(k < planes)
        def _():
            p = plane_at(k, z, planes)

            @pl.when(k > 0)
            def _():
                gather_copy(p * SEQS + place, y_s.at[p], at_y).wait_recv()

            start_all(forwards(p))

        j = k - lag

        @pl.when((j >= 0) & (j < planes))
        def _():
            p = plane_at(j, z, planes)
            second_forward(p).wait_recv()
            second_forward(p).start()
            pl.when(j == planes - 2)(lambda: core_sum(z))
            pl.when(j == planes - 1)(lambda: core_sum(plane_at(1, z, planes)))
            for row in range(2):
                gather_copy(p * SEQS + row * 2 + 1 - c, c_s.at[0], at_core).wait_recv()

            @pl.when(j == 0)
            def _():
                load_up.wait()
                load_down.wait()

            compute(p)
            for row in range(2):
                core_return(p, row).start()

        return carry

    lag = 1 + jnp.where(above & below, 1, 0)
    lax.fori_loop(0, planes + 2, advance, 0)
    def far_sum(i, carry):
        core_sum(plane_at(planes - 1 - i, z, planes))
        return carry

    lax.fori_loop(0, planes - 2, far_sum, 0)

    def chain(i, carry):
        p = plane_at(planes - 1 - i // HALVES, z, planes)
        h = i % HALVES
        y_return(p, h).wait_recv()
        own = piece(contrib, p * SEQS + place, h)
        terms = [own, piece(from_core, p * 2 + y, h), piece(from_y, p, h)]
        onward = ((p < z) & above) | ((p > z) & below)

        @pl.when(onward)
        def _():
            z_return(p, p, h, at_y).wait_recv()
            add_up(own, terms + [piece(from_z, p, h)])

        pl.when(jnp.logical_not(onward))(lambda: add_up(own, terms))

        @pl.when(p < z)
        def _():
            z_return(p, jnp.where(p == z - 1, planes, p), h, me - SEQS).start()

        @pl.when(p > z)
        def _():
            z_return(p, p, h, me + SEQS).start()

        return carry

    lax.fori_loop(0, (planes - 1) * HALVES, chain, 0)

    def last(h, carry):
        y_return(z, h).wait_recv()
        result = piece(out_ref, 0, h)
        terms = [
            piece(updated_ref, 0, h),
            piece(contrib, me, h),
            piece(from_core, z * 2 + y, h),
            piece(from_y, z, h),
        ]
        low, high = piece(from_z, z, h), piece(from_z, planes, h)
        pl.when(below)(lambda: z_return(z, z, h, at_y).wait_recv())
        pl.when(above)(lambda: z_return(z, planes, h, at_y).wait_recv())
        pl.when(below & above)(lambda: add_up(result, terms + [low, high]))
        pl.when(below & jnp.logical_not(above))(lambda: add_up(result, terms + [low]))
        pl.when(jnp.logical_not(below) & above)(lambda: add_up(result, terms + [high]))
        return carry

    lax.fori_loop(0, HALVES, last, 0)

    for by in range(1, planes):
        for copy in send_kv(by):
            copy.wait_send()
    tables_to_y().wait_send()
    tables_to_core().wait_send()

    def finish(p, carry):
        sent_all(column_forwards(p))
        pl.when(c == group)(column_seconds(p)[0].wait_send)
        column_seconds(p)[1].wait_send()
        sent_all(forwards(p))
        second_forward(p).wait_send()
        for row in range(2):
            core_return(p, row).wait_send()
        for h in range(HALVES):
            y_return(p, h).wait_send()

        @pl.when(p != z)
        def _():
            for h in range(HALVES):
                z_return(p, p, h, at_y).wait_send()

        return carry

    lax.fori_loop(0, planes, finish, 0)


def layer_call(
    order,
    residual,
    queries,
    keys,
    values,
    choices,
    gain,
    out_weight,
    w_gate_up,
    w_down,
    cap,
):
    n, width = residual.shape
    hidden = w_down.shape[1]
    devices = lax.axis_size("ctx")
    planes = devices // SEQS
    vmem = pl.BlockSpec(memory_space=pltpu.VMEM)
    anywhere = pl.BlockSpec(memory_space=pl.ANY)
    bf16 = jnp.bfloat16
    dma = pltpu.SemaphoreType.DMA
    return pl.pallas_call(
        functools.partial(layer_kernel, planes, cap),
        out_shape=[jax.ShapeDtypeStruct((n, width), bf16)] * 2,
        in_specs=[pl.BlockSpec(memory_space=pltpu.SMEM)] + [vmem] * 7 + [anywhere] * 2,
        out_specs=[vmem, vmem],
        scratch_shapes=[
            pltpu.VMEM((planes * n, 2 * keys.shape[1]), bf16),
            pltpu.VMEM((devices * devices, n), jnp.float32),
            pltpu.VMEM((2 * planes, 2 * n), jnp.float32),
            pltpu.VMEM((devices,) + out_weight.shape, bf16),
            pltpu.VMEM((n, width), jnp.float32),
            pltpu.VMEM((devices * n, width), bf16),
            pltpu.VMEM((devices * n, width), bf16),
            pltpu.VMEM((2 * planes * n, width), bf16),
            pltpu.VMEM((planes * n, width), bf16),
            pltpu.VMEM(((planes + 1) * n, width), bf16),
            pltpu.VMEM(w_gate_up.shape[1:], bf16),
            pltpu.VMEM(w_down.shape[1:], bf16),
            pltpu.VMEM((2 * planes, 2 * n), jnp.int32),
            pltpu.VMEM((SEQS * cap, width), bf16),
            pltpu.VMEM((SEQS * cap, hidden), bf16),
            dma((planes,)),
            dma((planes,)),
            dma((planes + 2,)),
            dma((planes + 2,)),
            dma((devices,)),
            dma((planes,)),
            dma((planes,)),
            dma((planes,)),
            dma((planes,)),
            dma((2 * planes,)),
            dma,
            dma((2,)),
            dma((devices,)),
            dma((planes,)),
            dma((planes,)),
            dma((planes,)),
            dma((2 * planes,)),
            dma((2 * planes,)),
            dma((2 * planes,)),
            dma((HALVES * planes,)),
            dma((HALVES * planes,)),
            dma((HALVES * planes,)),
            dma((HALVES * (planes + 1),)),
        ],
        compiler_params=pltpu.CompilerParams(
            collective_id=0, has_side_effects=True, vmem_limit_bytes=VMEM_BYTES
        ),
        name="layer",
    )(order, residual, queries, keys, values, choices, gain, out_weight, w_gate_up, w_down)


def fits(devices, rows, width, hidden):
    blocks = 4 * devices + 8
    if lax.axis_size("groups") != 2 or devices < 3 * SEQS:
        return False
    return 2 * (blocks * rows * width + 3 * width * hidden) < VMEM_BYTES * 4 // 5


def local(
    residual,
    queries,
    keys,
    values,
    block_order,
    routes,
    route_weights,
    out_weight,
    norm_gain,
    w_gate_up,
    w_down,
):
    device_row_count = queries.shape[0]
    query_group_width = QUERY_HEADS // KEY_VALUE_HEADS
    devices = lax.axis_size("ctx")
    cycle_length = devices // SEQS
    own_index = lax.axis_index("ctx")
    experts = devices * w_gate_up.shape[0]
    capacity = 9 * device_row_count * TOPK // (8 * experts)
    if fits(devices, device_row_count, D, FF):
        return tuple(
            layer_call(
                block_order,
                residual,
                queries,
                keys,
                values,
                jnp.concatenate([routes.astype(jnp.float32), route_weights], axis=1),
                norm_gain.reshape(1, -1),
                out_weight,
                w_gate_up,
                w_down,
                capacity,
            )
        )
    full_weight = lax.all_gather(out_weight, "ctx", axis=1, tiled=True)
    query_position = block_order[own_index]
    query_head_rows = (
        queries.reshape(device_row_count, KEY_VALUE_HEADS, query_group_width, HEAD_SIZE)
        .transpose(1, 2, 0, 3)
        .reshape(KEY_VALUE_HEADS, query_group_width * device_row_count, HEAD_SIZE)
    )
    query_offset = jnp.arange(query_group_width * device_row_count) % device_row_count
    key_offset = jnp.arange(device_row_count)
    scale = HEAD_SIZE ** (-0.5)

    def update(carry, key_value_tuple, key_position):
        summed, running_max, totals = carry
        local_key_block = key_value_tuple[0].reshape(device_row_count, KEY_VALUE_HEADS, HEAD_SIZE)
        local_value_block = key_value_tuple[1].reshape(device_row_count, KEY_VALUE_HEADS, HEAD_SIZE)
        scores = (
            jnp.einsum(
                "hqd,khd->hqk", query_head_rows, local_key_block, preferred_element_type=jnp.float32
            )
            * scale
        )
        visible = (
            key_position * device_row_count + key_offset[None, :]
            <= query_position * device_row_count + query_offset[:, None]
        )
        scores = jnp.where(visible[None], scores, -jnp.inf)
        new_max = jnp.maximum(running_max, jnp.max(scores, axis=-1))
        factor = jnp.exp(running_max - new_max)
        weights = jnp.exp(scores - new_max[..., None])
        totals = totals * factor + jnp.sum(weights, axis=-1)
        summed = summed * factor[..., None] + jnp.einsum(
            "hqk,khd->hqd",
            weights.astype(jnp.bfloat16),
            local_value_block,
            preferred_element_type=jnp.float32,
        )
        return (summed, new_max, totals)

    initial = (
        jnp.zeros((KEY_VALUE_HEADS, query_group_width * device_row_count, HEAD_SIZE), jnp.float32),
        jnp.full((KEY_VALUE_HEADS, query_group_width * device_row_count), -jnp.inf, jnp.float32),
        jnp.zeros((KEY_VALUE_HEADS, query_group_width * device_row_count), jnp.float32),
    )
    local_pair = jnp.stack([keys, values])
    carry = update(initial, local_pair, query_position)

    def advance(step, state):
        current, moving = state
        moving = shifted(moving, "ctx", SEQS)
        anchor = jnp.mod(own_index - SEQS * step, devices)
        key_position = block_order[anchor]
        current = lax.cond(
            key_position <= query_position,
            lambda inner: update(inner, moving, key_position),
            lambda inner: inner,
            current,
        )
        return (current, moving)

    carry, passed = lax.fori_loop(1, cycle_length, advance, (carry, local_pair))
    summed, running_max, totals = carry
    context = (
        (summed / totals[..., None])
        .reshape(KEY_VALUE_HEADS, query_group_width, device_row_count, HEAD_SIZE)
        .transpose(2, 0, 1, 3)
        .reshape(device_row_count, QUERY_HEADS * HEAD_SIZE)
        .astype(jnp.bfloat16)
    )
    projected = jnp.dot(context, full_weight, preferred_element_type=jnp.float32)
    updated = residual.astype(jnp.float32) + projected
    normed = (
        updated * lax.rsqrt(jnp.mean(updated * updated, axis=-1, keepdims=True) + 1e-06) * norm_gain
    ).astype(jnp.bfloat16)
    experts = devices * w_gate_up.shape[0]
    capacity = 9 * device_row_count * TOPK // (8 * experts)
    expert_ids = routes.reshape(-1)
    one_hot = (expert_ids[:, None] == jnp.arange(experts, dtype=jnp.int32)[None, :]).astype(
        jnp.int32
    )
    ranks = jnp.sum(jnp.cumsum(one_hot, axis=0) * one_hot, axis=1) - 1
    target = expert_ids * capacity + ranks
    source_row = jnp.arange(device_row_count * TOPK) // TOPK
    outgoing = (
        jnp.zeros((experts * capacity, D), jnp.bfloat16)
        .at[target]
        .set(normed[source_row])
        .reshape(experts, capacity, D)
    )
    arrived = lax.all_to_all(outgoing, "ctx", split_axis=0, concat_axis=0, tiled=True)
    flat = arrived.reshape(-1, D)
    both = jnp.dot(flat, w_gate_up[0], preferred_element_type=jnp.float32)
    hidden = (jax.nn.silu(both[:, :FF]) * both[:, FF:]).astype(jnp.bfloat16)
    result = (
        jnp.dot(hidden, w_down[0], preferred_element_type=jnp.float32)
        .astype(jnp.bfloat16)
        .reshape(arrived.shape)
    )
    returned = lax.all_to_all(result, "ctx", split_axis=0, concat_axis=0, tiled=True)
    gathered = returned.reshape(-1, D)[target].reshape(device_row_count, TOPK, D)
    gates = route_weights / jnp.sum(route_weights, axis=-1, keepdims=True)
    mixed = updated
    for slot in range(TOPK):
        mixed = mixed + gates[:, slot : slot + 1] * gathered[:, slot].astype(jnp.float32)
    return (context, mixed.astype(jnp.bfloat16))


def solution(mesh):
    placed = (
        P(("groups", "ctx"), None),
        P(("groups", "ctx"), None),
        P(("groups", "ctx"), None),
        P(("groups", "ctx"), None),
        P("groups"),
        P(("groups", "ctx"), None),
        P(("groups", "ctx"), None),
        P(None, "ctx"),
        P(),
        P("ctx", None, None),
        P("ctx", None, None),
    )
    return jax.shard_map(
        local,
        mesh=mesh,
        in_specs=placed,
        out_specs=(P(("groups", "ctx"), None), P(("groups", "ctx"), None)),
        check_vma=False,
    )
```
